512 devices in a mesh: dp: 128 (over x, z, core), outer: 4 (over y).
Axes of the slice: x: 4, y: 4, z: 16, core: 2. Of those that a mesh axis runs over, the one named last changes fastest.
Arguments:
- replica_grads: bfloat16 [128, 4, 128, 4608], P('dp', 'outer'), may hold values from -12 to 12, as said below
- hadamard_signs: int32 [256], replicated, may hold values from -1 to 1, as said below
- master_rows: float32 [128, 4608], P('dp'), may hold values from -0.3 to 0.3
- first_moment: float32 [128, 4608], P('dp'), may hold values from -6 to 6
- second_moment: float32 [128, 4608], P('dp'), may hold values from 0.5 to 4
Outputs:
- new_master: float32 [128, 4608], P('dp')
- new_first: float32 [128, 4608], P('dp')
- new_second: float32 [128, 4608], P('dp')
- updated_rows: bfloat16 [128, 4608], replicated
The draws below stay inside these ranges and needn't reach their ends.
Inputs may be any that keep to these rules, and one draw needn't show every extreme that they name: `hadamard_signs`: every entry is -1 or +1. `replica_grads`: every entry lies in the stated range on every mesh.
All inputs are finite; a program needn't handle non-finite values.
Results may differ from the reference program's by a relative error of at most 0.001.
Values may be sent and summed in bfloat16 or wider, within the bound.
A program may use at most 64 MiB of HBM per device.

```python
import math
import jax
import jax.numpy as jnp
from jax import lax

D = 4608
HAD = 256
STEP = 1000
ROWS = 128
BLOCKS = 18
N_DP = 128
N_OUTER = 4


def draw_hadamard_signs(key, part):
    key = jax.random.fold_in(key, 11)
    coins = jax.random.randint(key, (HAD,), 0, 2)
    return (2 * coins - 1).astype(jnp.int32)


def draw_replica_grads(key, part):
    key = jax.random.fold_in(key, 23)
    entry_key, scale_key = jax.random.split(key, 2)
    shape = (N_DP, N_OUTER, ROWS, D // HAD, HAD)
    log_scale = jnp.clip(jax.random.normal(scale_key, shape[:4], jnp.float32), -2.5, 2.5)
    block_scale = jnp.exp(1.5 * log_scale)
    entries = jnp.clip(jax.random.normal(entry_key, shape, jnp.float32), -6.0, 6.0)
    values = entries * block_scale[..., None] / jnp.sqrt(jnp.float32(N_DP * N_OUTER))
    values = jnp.clip(values, -12.0, 12.0)
    return values.reshape(N_DP, N_OUTER, ROWS, D).astype(jnp.bfloat16)


def draw_master_rows(key, part):
    key = jax.random.fold_in(key, 31)
    values = 0.05 * jnp.clip(jax.random.normal(key, (ROWS, D), jnp.float32), -6.0, 6.0)
    return values.astype(jnp.float32)


def steps_of(rng, dims, cuts, low, largest):
    factor_of, own = 1.0, jax.random.fold_in(rng, 6)
    for axis_at, shards_of in cuts:
        heights = jnp.exp(jax.random.uniform(jax.random.fold_in(own, axis_at), (shards_of,), jnp.float32, low / len(cuts), largest / len(cuts)))
        factor_of = factor_of * jnp.repeat(heights, dims[axis_at] // shards_of).reshape([-1 if axis == axis_at else 1 for axis in range(len(dims))])
    return factor_of


def gaussian(own_key, dims, width, most, shards=(), kind=jnp.bfloat16):
    result = jax.random.normal(own_key, dims, jnp.float32) * width
    if len(shards) > 0:
        result = steps_of(own_key, dims, shards, -0.22, 0.18) * result
    return jnp.clip(result, min=-most, max=most).astype(kind)


def setup_inputs(seed: int = 0) -> dict:
    seeds = jax.random.split(jax.random.key(seed), 6)
    replica_grads = draw_replica_grads(jax.random.fold_in(seeds[5], 71), 0)
    hadamard_signs = draw_hadamard_signs(jax.random.fold_in(seeds[5], 71), 0)
    master_rows = draw_master_rows(jax.random.fold_in(seeds[5], 71), 0)
    first_moment = gaussian(seeds[3], (ROWS, D), 1.0, 6.0, ((0, 128),), jnp.float32)
    second_moment = jnp.clip(jnp.exp(math.log(4.0) - 2.0794415 * jax.random.uniform(seeds[4], (ROWS, D), jnp.float32) ** steps_of(seeds[4], (ROWS, D), ((0, 128),), -0.2, 0.2)), 0.5, 4.0)
    return dict(replica_grads=replica_grads, hadamard_signs=hadamard_signs, master_rows=master_rows, first_moment=first_moment, second_moment=second_moment)


beta_one = 0.9
beta_two = 0.95
rate = 0.001
decay = 0.1
tiny_eps = 1e-08
clip_level = 1.5

def hadamard_table():
    indices = jnp.arange(HAD, dtype=jnp.int32)
    parity = jnp.zeros((HAD, HAD), jnp.int32)
    for bit_index in range(HAD.bit_length() - 1):
        column = jnp.bitwise_and(jnp.right_shift(indices, bit_index), 1)
        parity = parity + column[:, None] * column[None, :]
    return (1 - 2 * (parity % 2)).astype(jnp.float32)

def reference(replica_grads, hadamard_signs, master_rows, first_moment, second_moment):
    table = hadamard_table()
    table_half = table.astype(jnp.bfloat16)
    sign_half = hadamard_signs.astype(jnp.bfloat16)
    flat = replica_grads.reshape(N_DP * N_OUTER, ROWS * BLOCKS, HAD)

    def rotate(block_rows):
        signed = block_rows * sign_half[None, :]
        return jnp.dot(signed, table_half, preferred_element_type=jnp.float32) * 0.0625

    def peak_step(carry, block_rows):
        rotated = rotate(block_rows)
        return (jnp.maximum(carry, lax.optimization_barrier(jnp.mean(rotated * rotated, axis=1))), None)
    block_peak, _ = lax.scan(peak_step, jnp.zeros((ROWS * BLOCKS,), jnp.float32), flat)
    scales = jnp.sqrt(block_peak + 1e-06)

    def sum_step(carry, block_rows):
        rotated = rotate(block_rows)
        quantized = jnp.clip(rotated / scales[:, None], -clip_level, clip_level).astype(jnp.bfloat16)
        quantized = lax.optimization_barrier(quantized)
        return (carry + quantized.astype(jnp.float32), None)
    total, _ = lax.scan(sum_step, jnp.zeros((ROWS * BLOCKS, HAD), jnp.float32), flat)
    decoded = total * scales[:, None]
    gradient = jnp.dot(decoded, table, precision=lax.Precision.HIGHEST) * 0.0625
    gradient = (gradient * hadamard_signs.astype(jnp.float32)[None, :]).reshape(ROWS, D)
    new_first = beta_one * first_moment + (1.0 - beta_one) * gradient
    new_second = beta_two * second_moment + (1.0 - beta_two) * gradient * gradient
    first_fix = 1.0 - beta_one ** STEP
    second_fix = 1.0 - beta_two ** STEP
    update = new_first / first_fix / (jnp.sqrt(new_second / second_fix) + tiny_eps) + decay * master_rows
    new_master = master_rows - rate * update
    return (new_master, new_first, new_second, new_master.astype(jnp.bfloat16))
```

```python
import functools

import jax
import jax.numpy as jnp
from jax import lax
from jax.experimental import pallas as pl
from jax.experimental.pallas import tpu as pltpu
from jax.sharding import PartitionSpec as P

HAD = 256
LANES = 128
STEP = 1000
CORES = 2

beta_one = 0.9
beta_two = 0.95
rate = 0.001
decay = 0.1
tiny_eps = 1e-08
clip_level = 1.5
first_fix = 1.0 - beta_one**STEP
second_fix = 1.0 - beta_two**STEP

FIXED = 8192.0

F32 = jnp.float32
BF16 = jnp.bfloat16
MESH = pl.DeviceIdType.MESH


def ring_distance(offset, size):
    return min(offset, size - offset)


def hadamard(dtype):
    bits = lax.broadcasted_iota(jnp.int32, (HAD, HAD), 0) & lax.broadcasted_iota(
        jnp.int32, (HAD, HAD), 1
    )
    bits = bits ^ (bits >> 4)
    bits = bits ^ (bits >> 2)
    bits = bits ^ (bits >> 1)
    return (1 - 2 * (bits & 1)).astype(F32).astype(dtype)


def split_three(value):
    high = value.astype(BF16)
    rest = value - high.astype(F32)
    middle = rest.astype(BF16)
    low = (rest - middle.astype(F32)).astype(BF16)
    return high, middle, low


def dot(a, b):
    return jnp.dot(a, b, preferred_element_type=F32)


def kernel(
    sizes,
    grads_hbm,
    signs_ref,
    master_ref,
    first_ref,
    second_ref,
    new_master_ref,
    new_first_ref,
    new_second_ref,
    out_ref,
    x_ref,
    rot_ref,
    had_ref,
    perm_ref,
    adam_ref,
    ms_ref,
    ra_ref,
    vb_ref,
    rb_ref,
    vc_ref,
    rc_ref,
    peak_ref,
    inv_ref,
    col_ref,
    qs_ref,
    qr_ref,
    s_ref,
    rxy_ref,
    zs_ref,
    rz_ref,
    tot_ref,
    agz_ref,
    gb_ref,
    load_sem,
    send_sems,
    recv_sems,
):
    NX, NY, NZ, NB, W = sizes
    rows = NX * NZ * CORES
    half = NX * NZ
    HB = NB // 2

    dp = lax.axis_index("dp")
    y = lax.axis_index("outer")
    c = lax.rem(dp, CORES)
    z = lax.rem(dp // CORES, NZ)
    x = dp // (CORES * NZ)

    def first_block(at):
        return (at * (NB - W) + NY - 2) // (NY - 1)

    def device(dx, dy, dz, dc):
        px = lax.rem(x + dx, NX)
        py = lax.rem(y + dy, NY)
        pz = lax.rem(z + dz, NZ)
        pc = lax.rem(c + dc, CORES)
        return ((px * NZ + pz) * CORES + pc, py)

    plane = [(ox, oy) for oy in range(NY) for ox in range(NX) if ox or oy]
    plane.sort(key=lambda o: -(ring_distance(o[0], NX) + ring_distance(o[1], NY)))
    line = sorted(range(1, NZ), key=lambda o: -ring_distance(o, NZ))
    column = sorted(range(1, NY), key=lambda o: -ring_distance(o, NY))
    core_peer = device(0, 0, 0, 1)
    plane_peer = {o: device(o[0], o[1], 0, 0) for o in plane}
    line_peer = {o: device(0, 0, o, 0) for o in line}

    barrier = pltpu.get_barrier_semaphore()
    peers = [line_peer[o] for o in line] + [plane_peer[o] for o in plane] + [core_peer]
    for peer in peers:
        pl.semaphore_signal(barrier, inc=1, device_id=peer, device_id_type=MESH)

    load = pltpu.make_async_copy(grads_hbm.at[0, 0], x_ref, load_sem)
    load.start()

    counter = [0]
    pending = []

    def copy(src, dst, peer, index):
        return pltpu.make_async_remote_copy(
            src_ref=src,
            dst_ref=dst,
            send_sem=send_sems.at[index],
            recv_sem=recv_sems.at[index],
            device_id=peer,
            device_id_type=MESH,
        )

    def take(count):
        base = counter[0]
        counter[0] += count
        return base

    def start(src, dst, peer, index):
        descriptor = copy(src, dst, peer, index)
        descriptor.start()
        pending.append(descriptor)
        return descriptor

    had_ref[...] = hadamard(BF16)
    p_at = lax.broadcasted_iota(jnp.int32, (rows, rows), 0)
    r_at = lax.broadcasted_iota(jnp.int32, (rows, rows), 1)
    r_core = r_at % CORES
    r_pair = r_at // CORES
    perm = (p_at == r_core * half + r_pair).astype(F32)
    perm_ref[...] = perm
    for at in range(NY):
        for k in range(W):
            lo = (first_block(at) + k) * HAD
            adam_ref[0, at, k : k + 1, :] = master_ref[0:1, lo : lo + HAD]
            adam_ref[1, at, k : k + 1, :] = first_ref[0:1, lo : lo + HAD]
            adam_ref[2, at, k : k + 1, :] = second_ref[0:1, lo : lo + HAD]

    load.wait()

    lane = lax.broadcasted_iota(jnp.int32, (HAD, LANES), 1)
    sums = jnp.zeros((rows, LANES), F32)
    for block in range(NB):
        value = x_ref[:, block * HAD : (block + 1) * HAD].astype(F32)
        square = value * value
        high = square.astype(BF16)
        low = (square - high.astype(F32)).astype(BF16)
        pick = (lane == block).astype(F32).astype(BF16)
        sums = sums + (dot(high, pick) + dot(low, pick))
    means = jnp.transpose(sums) * (1.0 / HAD)
    ms_ref[0] = means[0:HB, :]
    ms_ref[1] = means[HB:NB, :]

    pl.semaphore_wait(barrier, len(peers))

    base = take(1)
    stage = start(ms_ref.at[1 - c], ra_ref, core_peer, base)
    stage.wait_recv()
    peak = jnp.maximum(ms_ref[c], ra_ref[...])
    vb_ref[...] = peak

    base = take(len(plane))
    stages = [
        start(vb_ref, rb_ref.at[j], plane_peer[o], base + j) for j, o in enumerate(plane)
    ]
    for j, stage in enumerate(stages):
        stage.wait_recv()
        peak = jnp.maximum(peak, rb_ref[j])
    vc_ref[...] = peak

    base = take(len(line))
    stages = [start(vc_ref, rc_ref.at[j], line_peer[o], base + j) for j, o in enumerate(line)]

    table = had_ref[...]
    order = perm.astype(BF16)
    signs = signs_ref[...].astype(F32).astype(BF16)
    for block in range(NB):
        cols = slice(block * HAD, (block + 1) * HAD)
        sorted_rows = dot(order, x_ref[:, cols]).astype(BF16)
        rotated = dot(sorted_rows * signs, table) * 0.0625
        rot_ref[0, :, cols] = rotated[0:half]
        rot_ref[1, :, cols] = rotated[half:rows]

    for j, stage in enumerate(stages):
        stage.wait_recv()
        peak = jnp.maximum(peak, rc_ref[j])
    peak_ref[c] = peak
    base = take(1)
    start(peak_ref.at[c], peak_ref.at[c], core_peer, base)
    copy(peak_ref.at[1 - c], peak_ref.at[1 - c], core_peer, base).wait_recv()

    scale_low = jnp.sqrt(peak_ref[0] + 1e-06)
    scale_high = jnp.sqrt(peak_ref[1] + 1e-06)
    scales = jnp.concatenate([scale_low, scale_high], axis=0)
    inv_ref[...] = jnp.zeros_like(inv_ref)
    inv_ref[0:NB, :] = 1.0 / scales
    inverse = lax.dot_general(
        perm_ref[...],
        inv_ref[...],
        (((1,), (1,)), ((), ())),
        precision=lax.Precision.HIGHEST,
        preferred_element_type=F32,
    )

    orders = [oy for oy in column] + [0]
    core_base = take(NY)
    plane_base = take(len(plane))

    def quantize(which, at):
        begin = first_block(at)
        cols = pl.ds(pl.multiple_of(begin * HAD, HAD), W * HAD)
        factors = pltpu.roll(inverse, lax.rem(LANES - begin, LANES), 1)
        value = rot_ref[which, :, cols]
        picked = jnp.where(which == 0, factors[0:half], factors[half:rows])
        return jnp.concatenate(
            [
                jnp.clip(
                    value[:, k * HAD : (k + 1) * HAD] * picked[:, k : k + 1],
                    -clip_level,
                    clip_level,
                ).astype(BF16)
                for k in range(W)
            ],
            axis=1,
        )

    core_stages = []
    for i, oy in enumerate(orders):
        at = lax.rem(y + oy, NY)
        qs_ref[i] = quantize(1 - c, at)
        core_stages.append(start(qs_ref.at[i], qr_ref.at[i], core_peer, core_base + i))

    plane_stages = {}
    for i, oy in enumerate(orders):
        at = lax.rem(y + oy, NY)
        own = quantize(c, at).astype(F32)
        core_stages[i].wait_recv()
        both = (own + qr_ref[i].astype(F32)) * FIXED
        coded = jnp.round(both).astype(jnp.int32).astype(jnp.int16)
        for px in range(NX):
            s_ref[i, px] = coded[px * NZ : (px + 1) * NZ]
        for j, o in enumerate(plane):
            if o[1] == oy:
                plane_stages[j] = start(
                    s_ref.at[i, lax.rem(x + o[0], NX)],
                    rxy_ref.at[j],
                    plane_peer[o],
                    plane_base + j,
                )

    row_lane = lax.broadcasted_iota(jnp.int32, (NB, rows), 1)
    own_scale = jnp.sum(jnp.where(row_lane == dp, scales, 0.0), axis=1, keepdims=True)
    own_scale = jnp.broadcast_to(own_scale, (NB, HAD))
    for at in range(NY):
        col_ref[at] = own_scale[first_block(at) : first_block(at) + W]

    total = s_ref[NY - 1, x].astype(jnp.int32)
    for j in sorted(plane_stages, key=lambda j: -j):
        plane_stages[j].wait_recv()
        total = total + rxy_ref[j].astype(jnp.int32)
    for k in range(W):
        for h in range(2):
            lo = k * HAD + h * LANES
            zs_ref[:, h * W + k, :] = total[:, lo : lo + LANES]

    base = take(len(line))
    stages = [
        start(zs_ref.at[lax.rem(z + o, NZ)], rz_ref.at[j], line_peer[o], base + j)
        for j, o in enumerate(line)
    ]
    total = zs_ref[z]
    for j in reversed(range(len(line))):
        stages[j].wait_recv()
        total = total + rz_ref[j]
    tot_ref[y] = total

    sign_row = signs_ref[...].astype(F32)

    def adam(summed, scale, master, first, second):
        parts = split_three(summed * scale)
        gradient = (dot(parts[0], table) + dot(parts[1], table)) + dot(parts[2], table)
        gradient = gradient * 0.0625 * sign_row
        new_first = beta_one * first + (1.0 - beta_one) * gradient
        new_second = beta_two * second + (1.0 - beta_two) * gradient * gradient
        update = (
            new_first * (1.0 / first_fix) / (jnp.sqrt(new_second * (1.0 / second_fix)) + tiny_eps)
            + decay * master
        )
        return master - rate * update, new_first, new_second

    def wide(value):
        value = value.astype(F32) * (1.0 / FIXED)
        return jnp.concatenate([value[0:W], value[W : 2 * W]], axis=1)

    updated, _, _ = adam(
        wide(total), col_ref[y], adam_ref[0, y], adam_ref[1, y], adam_ref[2, y]
    )
    updated = updated.astype(BF16).astype(F32)
    agz_ref[z, 0:W] = updated[:, 0:LANES]
    agz_ref[z, W : 2 * W] = updated[:, LANES:HAD]

    line_base = take(len(line))
    for j, o in enumerate(line):
        start(agz_ref.at[z], agz_ref.at[z], line_peer[o], line_base + j)
    column_base = take(len(column))
    for j, o in enumerate(column):
        start(tot_ref.at[y], tot_ref.at[y], plane_peer[(0, o)], column_base + j)

    for j, o in enumerate(column):
        source = lax.rem(y + NY - o, NY)
        copy(
            tot_ref.at[source], tot_ref.at[source], plane_peer[(0, o)], column_base + j
        ).wait_recv()
    for at in range(NY):
        results = adam(
            wide(tot_ref[at]), col_ref[at], adam_ref[0, at], adam_ref[1, at], adam_ref[2, at]
        )
        for ref, value in zip((new_master_ref, new_first_ref, new_second_ref), results):
            for k in range(W):
                lo = (first_block(at) + k) * HAD
                ref[0:1, lo : lo + HAD] = value[k : k + 1, :]

    for j, o in reversed(list(enumerate(line))):
        source = lax.rem(z + NZ - o, NZ)
        copy(agz_ref.at[source], agz_ref.at[source], line_peer[o], line_base + j).wait_recv()
    for k in range(W):
        for h in range(2):
            lo = k * HAD + h * LANES
            gb_ref[c, y, x, :, lo : lo + LANES] = agz_ref[:, h * W + k, :].astype(BF16)

    plane_base = take(len(plane))
    core_base = take(len(plane) + 1)
    for j, o in enumerate(plane):
        start(gb_ref.at[c, y, x], gb_ref.at[c, y, x], plane_peer[o], plane_base + j)
    start(gb_ref.at[c, y, x], gb_ref.at[c, y, x], core_peer, core_base + len(plane))
    for j, o in reversed(list(enumerate(plane))):
        sx = lax.rem(x + NX - o[0], NX)
        sy = lax.rem(y + NY - o[1], NY)
        here = gb_ref.at[c, sy, sx]
        copy(here, here, plane_peer[o], plane_base + j).wait_recv()
        start(here, here, core_peer, core_base + j)
    for j, o in list(enumerate(plane)) + [(len(plane), (0, 0))]:
        sx = lax.rem(x + NX - o[0], NX)
        sy = lax.rem(y + NY - o[1], NY)
        there = gb_ref.at[1 - c, sy, sx]
        copy(there, there, core_peer, core_base + j).wait_recv()

    back = jnp.transpose(perm_ref[...]).astype(BF16)
    done = 0
    for at in range(NY):
        skip = done - first_block(at)
        for k in range(skip, W):
            cols = slice(k * HAD, (k + 1) * HAD)
            block = jnp.concatenate(
                [
                    gb_ref[0, at, :, :, cols].reshape(half, HAD),
                    gb_ref[1, at, :, :, cols].reshape(half, HAD),
                ],
                axis=0,
            )
            lo = (first_block(at) + k) * HAD
            out_ref[:, lo : lo + HAD] = dot(back, block).astype(BF16)
        done = first_block(at) + W

    for descriptor in pending:
        descriptor.wait_send()


def build(mesh, NX, NZ, NB):
    NY = mesh.shape["outer"]
    W = -(-NB // NY)
    sizes = (NX, NY, NZ, NB, W)
    rows = NX * NZ * CORES
    half = NX * NZ
    HB = NB // 2
    n_plane = NX * NY - 1
    n_line = NZ - 1
    messages = 1 + n_plane + n_line + 1 + NY + n_plane + n_line
    messages += n_line + (NY - 1) + n_plane + n_plane + 1
    width = NB * HAD
    scratch = [
        pltpu.VMEM((rows, width), BF16),
        pltpu.VMEM((2, half, width), F32),
        pltpu.VMEM((HAD, HAD), BF16),
        pltpu.VMEM((rows, rows), F32),
        pltpu.VMEM((3, NY, W, HAD), F32),
        pltpu.VMEM((2, HB, rows), F32),
        pltpu.VMEM((HB, rows), F32),
        pltpu.VMEM((HB, rows), F32),
        pltpu.VMEM((n_plane, HB, rows), F32),
        pltpu.VMEM((HB, rows), F32),
        pltpu.VMEM((n_line, HB, rows), F32),
        pltpu.VMEM((2, HB, rows), F32),
        pltpu.VMEM((LANES, rows), F32),
        pltpu.VMEM((NY, W, HAD), F32),
        pltpu.VMEM((NY, half, W * HAD), BF16),
        pltpu.VMEM((NY, half, W * HAD), BF16),
        pltpu.VMEM((NY, NX, NZ, W * HAD), jnp.int16),
        pltpu.VMEM((n_plane, NZ, W * HAD), jnp.int16),
        pltpu.VMEM((NZ, 2 * W, LANES), jnp.int32),
        pltpu.VMEM((n_line, 2 * W, LANES), jnp.int32),
        pltpu.VMEM((NY, 2 * W, LANES), jnp.int32),
        pltpu.VMEM((NZ, 2 * W, LANES), F32),
        pltpu.VMEM((2, NY, NX, NZ, W * HAD), BF16),
        pltpu.SemaphoreType.DMA,
        pltpu.SemaphoreType.DMA((messages,)),
        pltpu.SemaphoreType.DMA((messages,)),
    ]
    vmem = pl.BlockSpec(memory_space=pltpu.VMEM)
    row = jax.ShapeDtypeStruct((1, width), F32)

    def per_device(replica_grads, hadamard_signs, master_rows, first_moment, second_moment):
        return pl.pallas_call(
            functools.partial(kernel, sizes),
            out_shape=(row, row, row, jax.ShapeDtypeStruct((rows, width), BF16)),
            in_specs=[pl.BlockSpec(memory_space=pl.ANY)] + [vmem] * 4,
            out_specs=(vmem, vmem, vmem, vmem),
            scratch_shapes=scratch,
            compiler_params=pltpu.CompilerParams(
                collective_id=0, has_side_effects=True, vmem_limit_bytes=56 * 2**20
            ),
        )(
            replica_grads,
            hadamard_signs.reshape(1, HAD),
            master_rows,
            first_moment,
            second_moment,
        )

    in_specs = (P("dp", "outer", None, None), P(), P("dp", None), P("dp", None), P("dp", None))
    out_specs = (P("dp", None), P("dp", None), P("dp", None), P())
    return jax.shard_map(
        per_device, mesh=mesh, in_specs=in_specs, out_specs=out_specs, check_vma=False
    )


def solution(mesh):
    return build(mesh, 4, 16, 18)
```

```python
import functools

import jax
import jax.numpy as jnp
from jax import lax
from jax.experimental import pallas as pl
from jax.experimental.pallas import tpu as pltpu
from jax.sharding import PartitionSpec as P

HAD = 256
LANES = 128
STEP = 1000
CORES = 2

beta_one = 0.9
beta_two = 0.95
rate = 0.001
decay = 0.1
tiny_eps = 1e-08
clip_level = 1.5
first_fix = 1.0 - beta_one**STEP
second_fix = 1.0 - beta_two**STEP

F32 = jnp.float32
BF16 = jnp.bfloat16
MESH = pl.DeviceIdType.MESH


def ring_distance(offset, size):
    return min(offset, size - offset)


def hadamard(dtype):
    bits = lax.broadcasted_iota(jnp.int32, (HAD, HAD), 0) & lax.broadcasted_iota(
        jnp.int32, (HAD, HAD), 1
    )
    bits = bits ^ (bits >> 4)
    bits = bits ^ (bits >> 2)
    bits = bits ^ (bits >> 1)
    return (1 - 2 * (bits & 1)).astype(F32).astype(dtype)


def split_three(value):
    high = value.astype(BF16)
    rest = value - high.astype(F32)
    middle = rest.astype(BF16)
    low = (rest - middle.astype(F32)).astype(BF16)
    return high, middle, low


def dot(a, b):
    return jnp.dot(a, b, preferred_element_type=F32)


def adam(gradient, master, first, second):
    new_first = beta_one * first + (1.0 - beta_one) * gradient
    new_second = beta_two * second + (1.0 - beta_two) * gradient * gradient
    update = (
        new_first * (1.0 / first_fix) / (jnp.sqrt(new_second * (1.0 / second_fix)) + tiny_eps)
        + decay * master
    )
    return master - rate * update, new_first, new_second


def piece_start(sizes, at):
    NX, NY, NZ, NB, W = sizes
    return (at * (NB - W) + NY - 2) // (NY - 1)


def exchange_kernel(
    sizes,
    grads_hbm,
    signs_ref,
    master_ref,
    first_ref,
    second_ref,
    gb_ref,
    grad_ref,
    x_ref,
    table_ref,
    signed_ref,
    adam_ref,
    bulk_ref,
    rbulk_ref,
    rot_ref,
    m1_ref,
    r1_ref,
    m2_ref,
    r2_ref,
    m3_ref,
    r3_ref,
    acc_ref,
    racc_ref,
    zs_ref,
    rz_ref,
    agz_ref,
    load_sem,
    send_sems,
    recv_sems,
):
    NX, NY, NZ, NB, W = sizes
    rows = NX * NZ * CORES
    pair = CORES * NZ
    stride = LANES // NZ

    dp = lax.axis_index("dp")
    y = lax.axis_index("outer")
    c = lax.rem(dp, CORES)
    z = lax.rem(dp // CORES, NZ)
    x = dp // (CORES * NZ)

    def first_block(at):
        return piece_start(sizes, at)

    def device(dx, dy, dz, dc):
        px = lax.rem(x + dx, NX)
        py = lax.rem(y + dy, NY)
        pz = lax.rem(z + dz, NZ)
        pc = lax.rem(c + dc, CORES)
        return ((px * NZ + pz) * CORES + pc, py)

    def hops(o):
        return ring_distance(o[0], NX) + ring_distance(o[1], NY)

    plane = [(ox, oy) for oy in range(NY) for ox in range(NX) if ox or oy]
    plane.sort(key=lambda o: -hops(o))
    line = sorted(range(1, NZ), key=lambda o: -ring_distance(o, NZ))
    column = sorted(range(1, NY), key=lambda o: -ring_distance(o, NY))
    core_peer = device(0, 0, 0, 1)
    plane_peer = [device(o[0], o[1], 0, 0) for o in plane]
    line_peer = [device(0, 0, o, 0) for o in line]
    here = len(plane)

    barrier = pltpu.get_barrier_semaphore()
    peers = line_peer + plane_peer + [core_peer]
    for peer in peers:
        pl.semaphore_signal(barrier, inc=1, device_id=peer, device_id_type=MESH)

    load = pltpu.make_async_copy(grads_hbm.at[0, 0], x_ref, load_sem)
    load.start()

    counter = [0]
    pending = []

    def copy(src, dst, peer, index):
        return pltpu.make_async_remote_copy(
            src_ref=src,
            dst_ref=dst,
            send_sem=send_sems.at[index],
            recv_sem=recv_sems.at[index],
            device_id=peer,
            device_id_type=MESH,
        )

    def take(count):
        base = counter[0]
        counter[0] += count
        return base

    def start(src, dst, peer, index):
        descriptor = copy(src, dst, peer, index)
        descriptor.start()
        pending.append(descriptor)
        return descriptor

    p_at = lax.broadcasted_iota(jnp.int32, (rows, rows), 0)
    r_at = lax.broadcasted_iota(jnp.int32, (rows, rows), 1)
    r_core = r_at % CORES
    r_z = (r_at // CORES) % NZ
    r_x = r_at // pair
    order = (p_at == r_x * pair + r_core * NZ + r_z).astype(F32).astype(BF16)

    table = hadamard(BF16)
    table_ref[...] = table

    load.wait()

    lane = lax.broadcasted_iota(jnp.int32, (HAD, LANES), 1)
    picks = [(lane % stride == k).astype(F32).astype(BF16) for k in range(W)]
    sums = [jnp.zeros((rows, LANES), F32) for _ in range(NY)]
    for block in range(NB):
        value = dot(order, x_ref[:, block * HAD : (block + 1) * HAD])
        square = value * value
        high = square.astype(BF16)
        low = (square - high.astype(F32)).astype(BF16)
        both = jnp.concatenate([high, low], axis=0)
        value = value.astype(BF16).reshape(NX, pair, HAD)
        for at in range(NY):
            k = block - first_block(at)
            if 0 <= k < W:
                part = dot(both, picks[k])
                sums[at] = sums[at] + (part[0:rows] + part[rows : 2 * rows])
                bulk_ref[at, :, :, k * HAD : (k + 1) * HAD] = value
    row_at = lax.broadcasted_iota(jnp.int32, (rows, LANES), 0)
    lane_at = lax.broadcasted_iota(jnp.int32, (rows, LANES), 1)
    mine = row_at % NZ == lane_at // stride
    for at in range(NY):
        packed = jnp.where(mine, sums[at], 0.0).reshape(NX * CORES, NZ, LANES)
        packed = jnp.sum(packed, axis=1) * (1.0 / HAD)
        for px in range(NX):
            m1_ref[at, px] = packed[px * CORES : (px + 1) * CORES]

    pl.semaphore_wait(barrier, len(peers))

    base = take(here)
    stages = []
    for j, o in enumerate(plane):
        piece = m1_ref.at[lax.rem(y + o[1], NY), lax.rem(x + o[0], NX)]
        stages.append(start(piece, r1_ref.at[j], plane_peer[j], base + j))
    base = take(here)
    bulk_stages = []
    for j, o in enumerate(plane):
        piece = bulk_ref.at[lax.rem(y + o[1], NY), lax.rem(x + o[0], NX)]
        bulk_stages.append(start(piece, rbulk_ref.at[j], plane_peer[j], base + j))
    rbulk_ref[here] = bulk_ref[y, x]

    diagonal = lax.broadcasted_iota(jnp.int32, (HAD, HAD), 0) == lax.broadcasted_iota(
        jnp.int32, (HAD, HAD), 1
    )
    sign_row = signs_ref[...].astype(F32)
    signed_ref[...] = dot(
        jnp.where(diagonal, sign_row, 0.0).astype(BF16), table
    ).astype(BF16)
    for at in range(NY):
        for k in range(W):
            lo = (first_block(at) + k) * HAD
            adam_ref[0, at, k : k + 1, :] = master_ref[0:1, lo : lo + HAD]
            adam_ref[1, at, k : k + 1, :] = first_ref[0:1, lo : lo + HAD]
            adam_ref[2, at, k : k + 1, :] = second_ref[0:1, lo : lo + HAD]

    peak = m1_ref[y, x]
    for j in reversed(range(here)):
        stages[j].wait_recv()
        peak = jnp.maximum(peak, r1_ref[j])
    m2_ref[...] = peak
    base = take(1)
    start(m2_ref, r2_ref, core_peer, base).wait_recv()
    peak = jnp.maximum(peak, r2_ref[...])
    m3_ref[...] = peak
    base = take(len(line))
    stages = [start(m3_ref, r3_ref.at[j], line_peer[j], base + j) for j in range(len(line))]

    signed = signed_ref[...]
    far = len([o for o in plane if hops(o) > 2])
    for lo_slot, hi_slot in ((far, here + 1), (0, far)):
        count = hi_slot - lo_slot
        if count == 0:
            continue
        for j in reversed(range(lo_slot, min(hi_slot, here))):
            bulk_stages[j].wait_recv()
        for k in range(W):
            cols = slice(k * HAD, (k + 1) * HAD)
            value = rbulk_ref[lo_slot:hi_slot, :, cols].reshape(count * pair, HAD)
            rot_ref[lo_slot:hi_slot, :, cols] = dot(value, signed).reshape(count, pair, HAD)

    for j in reversed(range(len(line))):
        stages[j].wait_recv()
        peak = jnp.maximum(peak, r3_ref[j])

    scales = jnp.sqrt(peak + 1e-06)
    inverse = 0.0625 / scales
    z_at = lax.broadcasted_iota(jnp.int32, (NZ, LANES), 0)
    l_at = lax.broadcasted_iota(jnp.int32, (NZ, LANES), 1)
    base = take(W)
    core_stages = []
    for k in range(W):
        cols = slice(k * HAD, (k + 1) * HAD)
        pick = l_at == z_at * stride + k
        factor = jnp.concatenate(
            [
                jnp.sum(
                    jnp.where(pick, jnp.broadcast_to(inverse[g : g + 1], (NZ, LANES)), 0.0),
                    axis=1,
                    keepdims=True,
                )
                for g in range(CORES)
            ],
            axis=0,
        )
        factor = jnp.broadcast_to(factor, (pair, HAD))
        total = jnp.zeros((pair, HAD), F32)
        for j in range(here + 1):
            value = jnp.clip(rot_ref[j, :, cols] * factor, -clip_level, clip_level)
            total = total + value.astype(BF16).astype(F32)
        acc_ref[0, :, cols] = total[0:NZ]
        acc_ref[1, :, cols] = total[NZ:pair]
        core_stages.append(
            start(acc_ref.at[1 - c, :, cols], racc_ref.at[:, cols], core_peer, base + k)
        )

    w_at = lax.broadcasted_iota(jnp.int32, (W, LANES), 0)
    k_at = lax.broadcasted_iota(jnp.int32, (W, LANES), 1)
    own = jnp.broadcast_to(jnp.where(c == 0, scales[0:1], scales[1:2]), (W, LANES))
    own_scale = jnp.sum(
        jnp.where(k_at == z * stride + w_at, own, 0.0), axis=1, keepdims=True
    )

    for k in range(W):
        core_stages[k].wait_recv()
        for h in range(2):
            cols = slice(k * HAD + h * LANES, k * HAD + (h + 1) * LANES)
            zs_ref[:, h * W + k, :] = acc_ref[c, :, cols] + racc_ref[:, cols]

    base = take(len(line))
    stages = [
        start(zs_ref.at[lax.rem(z + o, NZ)], rz_ref.at[j], line_peer[j], base + j)
        for j, o in enumerate(line)
    ]
    total = zs_ref[z]
    for j in reversed(range(len(line))):
        stages[j].wait_recv()
        total = total + rz_ref[j]

    wide = jnp.concatenate([total[0:W], total[W : 2 * W]], axis=1)
    parts = split_three(wide * own_scale)
    table = table_ref[...]
    gradient = (dot(parts[0], table) + dot(parts[1], table)) + dot(parts[2], table)
    gradient = gradient * 0.0625 * sign_row
    grad_ref[y] = gradient
    updated, _, _ = adam(gradient, adam_ref[0, y], adam_ref[1, y], adam_ref[2, y])
    updated = updated.astype(BF16).astype(F32)
    agz_ref[z, 0:W] = updated[:, 0:LANES]
    agz_ref[z, W : 2 * W] = updated[:, LANES:HAD]

    base = take(len(line))
    for j in range(len(line)):
        start(agz_ref.at[z], agz_ref.at[z], line_peer[j], base + j)
    column_base = take(len(column))
    for j, o in enumerate(column):
        start(grad_ref.at[y], grad_ref.at[y], device(0, o, 0, 0), column_base + j)
    for j in reversed(range(len(line))):
        source = agz_ref.at[lax.rem(z + NZ - line[j], NZ)]
        copy(source, source, line_peer[j], base + j).wait_recv()
    for k in range(W):
        for h in range(2):
            lo = k * HAD + h * LANES
            gb_ref[c, y, x, :, lo : lo + LANES] = agz_ref[:, h * W + k, :].astype(BF16)

    plane_base = take(here)
    core_base = take(here + 1)
    piece = gb_ref.at[c, y, x]
    for j in range(here):
        start(piece, piece, plane_peer[j], plane_base + j)
    start(piece, piece, core_peer, core_base + here)
    sources = [
        (lax.rem(y + NY - o[1], NY), lax.rem(x + NX - o[0], NX)) for o in plane + [(0, 0)]
    ]
    for j in reversed(range(here)):
        piece = gb_ref.at[c, sources[j][0], sources[j][1]]
        copy(piece, piece, plane_peer[j], plane_base + j).wait_recv()
        start(piece, piece, core_peer, core_base + j)
    for j in reversed(range(here + 1)):
        piece = gb_ref.at[1 - c, sources[j][0], sources[j][1]]
        copy(piece, piece, core_peer, core_base + j).wait_recv()
    for j, o in enumerate(column):
        source = grad_ref.at[lax.rem(y + NY - o, NY)]
        copy(source, source, device(0, o, 0, 0), column_base + j).wait_recv()

    for descriptor in pending:
        descriptor.wait_send()


def write_kernel(
    sizes,
    gb_ref,
    grad_ref,
    master_ref,
    first_ref,
    second_ref,
    new_master_ref,
    new_first_ref,
    new_second_ref,
    out_ref,
    adam_ref,
):
    NX, NY, NZ, NB, W = sizes
    rows = NX * NZ * CORES
    half = NX * NZ
    r_at = lax.broadcasted_iota(jnp.int32, (rows, rows), 0)
    p_at = lax.broadcasted_iota(jnp.int32, (rows, rows), 1)
    back = (p_at == (r_at % CORES) * half + r_at // CORES).astype(F32).astype(BF16)
    done = 0
    for at in range(NY):
        begin = piece_start(sizes, at)
        for k in range(W):
            lo = (begin + k) * HAD
            adam_ref[0, k : k + 1, :] = master_ref[0:1, lo : lo + HAD]
            adam_ref[1, k : k + 1, :] = first_ref[0:1, lo : lo + HAD]
            adam_ref[2, k : k + 1, :] = second_ref[0:1, lo : lo + HAD]
        results = adam(grad_ref[at], adam_ref[0], adam_ref[1], adam_ref[2])
        for k in range(done - begin, W):
            lo = (begin + k) * HAD
            for ref, value in zip((new_master_ref, new_first_ref, new_second_ref), results):
                ref[0:1, lo : lo + HAD] = value[k : k + 1, :]
            cols = slice(k * HAD, (k + 1) * HAD)
            block = gb_ref[:, at, :, :, cols].reshape(rows, HAD)
            out_ref[:, lo : lo + HAD] = dot(back, block).astype(BF16)
        done = begin + W


def build(mesh, NX, NZ, NB):
    NY = mesh.shape["outer"]
    W = -(-NB // NY)
    sizes = (NX, NY, NZ, NB, W)
    rows = NX * NZ * CORES
    pair = CORES * NZ
    n_plane = NX * NY - 1
    n_line = NZ - 1
    messages = n_plane + n_plane + 1 + n_line + W + n_line
    messages += n_line + (NY - 1) + n_plane + n_plane + 1
    width = NB * HAD
    piece = W * HAD
    scratch = [
        pltpu.VMEM((rows, width), BF16),
        pltpu.VMEM((HAD, HAD), BF16),
        pltpu.VMEM((HAD, HAD), BF16),
        pltpu.VMEM((3, NY, W, HAD), F32),
        pltpu.VMEM((NY, NX, pair, piece), BF16),
        pltpu.VMEM((n_plane + 1, pair, piece), BF16),
        pltpu.VMEM((n_plane + 1, pair, piece), F32),
        pltpu.VMEM((NY, NX, CORES, LANES), F32),
        pltpu.VMEM((n_plane, CORES, LANES), F32),
        pltpu.VMEM((CORES, LANES), F32),
        pltpu.VMEM((CORES, LANES), F32),
        pltpu.VMEM((CORES, LANES), F32),
        pltpu.VMEM((n_line, CORES, LANES), F32),
        pltpu.VMEM((CORES, NZ, piece), F32),
        pltpu.VMEM((NZ, piece), F32),
        pltpu.VMEM((NZ, 2 * W, LANES), F32),
        pltpu.VMEM((n_line, 2 * W, LANES), F32),
        pltpu.VMEM((NZ, 2 * W, LANES), F32),
        pltpu.SemaphoreType.DMA,
        pltpu.SemaphoreType.DMA((messages,)),
        pltpu.SemaphoreType.DMA((messages,)),
    ]
    vmem = pl.BlockSpec(memory_space=pltpu.VMEM)
    row = jax.ShapeDtypeStruct((1, width), F32)

    def per_device(replica_grads, hadamard_signs, master_rows, first_moment, second_moment):
        gathered, gradients = pl.pallas_call(
            functools.partial(exchange_kernel, sizes),
            out_shape=(
                jax.ShapeDtypeStruct((CORES, NY, NX, NZ, piece), BF16),
                jax.ShapeDtypeStruct((NY, W, HAD), F32),
            ),
            in_specs=[pl.BlockSpec(memory_space=pltpu.HBM)] + [vmem] * 4,
            out_specs=(vmem, vmem),
            scratch_shapes=scratch,
            compiler_params=pltpu.CompilerParams(
                collective_id=0, has_side_effects=True, vmem_limit_bytes=40 * 2**20
            ),
        )(
            replica_grads,
            hadamard_signs.reshape(1, HAD),
            master_rows,
            first_moment,
            second_moment,
        )
        return pl.pallas_call(
            functools.partial(write_kernel, sizes),
            out_shape=(row, row, row, jax.ShapeDtypeStruct((rows, width), BF16)),
            in_specs=[vmem] * 5,
            out_specs=(vmem,) * 4,
            scratch_shapes=[pltpu.VMEM((3, W, HAD), F32)],
            compiler_params=pltpu.CompilerParams(vmem_limit_bytes=20 * 2**20),
        )(gathered, gradients, master_rows, first_moment, second_moment)

    in_specs = (P("dp", "outer", None, None), P(), P("dp", None), P("dp", None), P("dp", None))
    out_specs = (P("dp", None), P("dp", None), P("dp", None), P())
    return jax.shard_map(
        per_device, mesh=mesh, in_specs=in_specs, out_specs=out_specs, check_vma=False
    )


def solution(mesh):
    return build(mesh, 4, 16, 18)
```

```python
import functools

import jax
import jax.numpy as jnp
from jax import lax
from jax.experimental import pallas as pl
from jax.experimental.pallas import tpu as pltpu
from jax.sharding import PartitionSpec as P

HAD = 256
LANES = 128
STEP = 1000
CORES = 2

beta_one = 0.9
beta_two = 0.95
rate = 0.001
decay = 0.1
tiny_eps = 1e-08
clip_level = 1.5
first_fix = 1.0 - beta_one**STEP
second_fix = 1.0 - beta_two**STEP

F32 = jnp.float32
BF16 = jnp.bfloat16
MESH = pl.DeviceIdType.MESH


def ring_distance(offset, size):
    return min(offset, size - offset)


def hadamard(dtype):
    bits = lax.broadcasted_iota(jnp.int32, (HAD, HAD), 0) & lax.broadcasted_iota(
        jnp.int32, (HAD, HAD), 1
    )
    bits = bits ^ (bits >> 4)
    bits = bits ^ (bits >> 2)
    bits = bits ^ (bits >> 1)
    return (1 - 2 * (bits & 1)).astype(F32).astype(dtype)


def split_three(value):
    high = value.astype(BF16)
    rest = value - high.astype(F32)
    middle = rest.astype(BF16)
    low = (rest - middle.astype(F32)).astype(BF16)
    return high, middle, low


def dot(a, b):
    return jnp.dot(a, b, preferred_element_type=F32)


def adam(gradient, master, first, second):
    new_first = beta_one * first + (1.0 - beta_one) * gradient
    new_second = beta_two * second + (1.0 - beta_two) * gradient * gradient
    update = (
        new_first * (1.0 / first_fix) / (jnp.sqrt(new_second * (1.0 / second_fix)) + tiny_eps)
        + decay * master
    )
    return master - rate * update, new_first, new_second


def piece_start(sizes, at):
    NX, NY, NZ, NB, W = sizes
    return (at * (NB - W) + NY - 2) // (NY - 1)


def plane_offsets(NX, NY):
    plane = [(ox, oy) for oy in range(NY) for ox in range(NX) if ox or oy]
    return sorted(plane, key=lambda o: -plane_hops(NX, NY, o))


def plane_hops(NX, NY, o):
    return ring_distance(o[0], NX) + ring_distance(o[1], NY)


def line_offsets(NZ):
    back = max(NZ // 4 - 1, 0)
    near = [o for o in range(-back, NZ // 2 - back) if o]
    far = list(range(NZ // 2 - back, NZ - back))
    return near, far


def exchange_kernel(
    sizes,
    grads_hbm,
    signs_hbm,
    master_hbm,
    first_hbm,
    second_hbm,
    gb_ref,
    grad_ref,
    x_ref,
    signs_ref,
    state_ref,
    table_ref,
    signed_ref,
    adam_ref,
    bulka_ref,
    bulkb_ref,
    rbulka_ref,
    rbulkb_ref,
    rota_ref,
    rotb_ref,
    m1_ref,
    r1_ref,
    m2_ref,
    r2_ref,
    m3_ref,
    r3_ref,
    acc_ref,
    racc_ref,
    zs_ref,
    rz_ref,
    near_ref,
    far_ref,
    load_sems,
    send_sems,
    recv_sems,
):
    NX, NY, NZ, NB, W = sizes
    rows = NX * NZ * CORES
    pair = CORES * NZ
    stride = LANES // NZ

    dp = lax.axis_index("dp")
    y = lax.axis_index("outer")
    c = lax.rem(dp, CORES)
    z = lax.rem(dp // CORES, NZ)
    x = dp // (CORES * NZ)

    def first_block(at):
        return piece_start(sizes, at)

    def device(dx, dy, dz, dc):
        px = lax.rem(x + dx, NX)
        py = lax.rem(y + dy, NY)
        pz = lax.rem(z + dz, NZ)
        pc = lax.rem(c + dc, CORES)
        return ((px * NZ + pz) * CORES + pc, py)

    plane = plane_offsets(NX, NY)
    near, far = line_offsets(NZ)
    line = sorted([o % NZ for o in near + far], key=lambda o: -ring_distance(o, NZ))
    column = list(range(1, NY))
    core_peer = device(0, 0, 0, 1)
    plane_peer = [device(o[0], o[1], 0, 0) for o in plane]
    line_peer = {o: device(0, 0, o, 0) for o in line}
    here = len(plane)
    WA = (W + 1) // 2

    barrier = pltpu.get_barrier_semaphore()
    peers = [line_peer[o] for o in line] + plane_peer + [core_peer]
    for peer in peers:
        pl.semaphore_signal(barrier, inc=1, device_id=peer, device_id_type=MESH)

    begin = pl.multiple_of(first_block(y) * HAD, HAD)
    loads = [
        pltpu.make_async_copy(grads_hbm.at[0, 0], x_ref, load_sems.at[0]),
        pltpu.make_async_copy(signs_hbm, signs_ref, load_sems.at[1]),
    ]
    for i, hbm in enumerate((master_hbm, first_hbm, second_hbm)):
        loads.append(
            pltpu.make_async_copy(
                hbm.at[:, pl.ds(begin, W * HAD)], state_ref.at[i], load_sems.at[2 + i]
            )
        )
    for load in loads:
        load.start()

    counter = [0]
    sent = []

    def copy(src, dst, peer, send, recv):
        return pltpu.make_async_remote_copy(
            src_ref=src,
            dst_ref=dst,
            send_sem=send_sems.at[send],
            recv_sem=recv_sems.at[recv],
            device_id=peer,
            device_id_type=MESH,
        )

    def stage():
        counter[0] += 1
        return counter[0] - 1

    def landed(ref, index):
        copy(ref, ref, core_peer, index, index).wait_recv()

    p_at = lax.broadcasted_iota(jnp.int32, (rows, rows), 0)
    r_at = lax.broadcasted_iota(jnp.int32, (rows, rows), 1)
    r_core = r_at % CORES
    r_z = (r_at // CORES) % NZ
    r_x = r_at // pair
    order = (p_at == r_x * pair + r_core * NZ + r_z).astype(F32).astype(BF16)

    table = hadamard(BF16)
    table_ref[...] = table

    loads[0].wait()

    lane = lax.broadcasted_iota(jnp.int32, (HAD, LANES), 1)
    picks = [(lane % stride == k).astype(F32).astype(BF16) for k in range(W)]
    sums = [jnp.zeros((rows, LANES), F32) for _ in range(NY)]
    for block in range(NB):
        value = dot(order, x_ref[:, block * HAD : (block + 1) * HAD])
        square = value * value
        high = square.astype(BF16)
        low = (square - high.astype(F32)).astype(BF16)
        both = jnp.concatenate([high, low], axis=0)
        value = value.astype(BF16).reshape(NX, pair, HAD)
        for at in range(NY):
            k = block - first_block(at)
            if 0 <= k < W:
                part = dot(both, picks[k])
                sums[at] = sums[at] + (part[0:rows] + part[rows : 2 * rows])
                if k < WA:
                    bulka_ref[at, :, :, k * HAD : (k + 1) * HAD] = value
                else:
                    bulkb_ref[at, :, :, (k - WA) * HAD : (k - WA + 1) * HAD] = value
    row_at = lax.broadcasted_iota(jnp.int32, (rows, LANES), 0)
    lane_at = lax.broadcasted_iota(jnp.int32, (rows, LANES), 1)
    mine = row_at % NZ == lane_at // stride
    for at in range(NY):
        packed = jnp.where(mine, sums[at], 0.0).reshape(NX * CORES, NZ, LANES)
        packed = jnp.sum(packed, axis=1) * (1.0 / HAD)
        for px in range(NX):
            m1_ref[at, px] = packed[px * CORES : (px + 1) * CORES]

    pl.semaphore_wait(barrier, len(peers))

    def over_plane(parts_ref, slots_ref):
        index = stage()
        for j, o in enumerate(plane):
            piece = parts_ref.at[lax.rem(y + o[1], NY), lax.rem(x + o[0], NX)]
            copy(piece, slots_ref.at[j], plane_peer[j], index, index).start()
        sent.append((slots_ref.at[0:here], index))
        return index

    first_maxima = over_plane(m1_ref, r1_ref)
    wave_a = over_plane(bulka_ref, rbulka_ref)
    rbulka_ref[here] = bulka_ref[y, x]
    rbulkb_ref[here] = bulkb_ref[y, x]

    diagonal = lax.broadcasted_iota(jnp.int32, (HAD, HAD), 0) == lax.broadcasted_iota(
        jnp.int32, (HAD, HAD), 1
    )
    for load in loads[1:]:
        load.wait()
    sign_row = signs_ref[...].astype(F32)
    signed_ref[...] = dot(
        jnp.where(diagonal, sign_row, 0.0).astype(BF16), table
    ).astype(BF16)
    for k in range(W):
        for i in range(3):
            adam_ref[i, k : k + 1, :] = state_ref[i, :, k * HAD : (k + 1) * HAD]

    landed(r1_ref, first_maxima)
    peak = jnp.maximum(m1_ref[y, x], jnp.max(r1_ref[...], axis=0))
    m2_ref[...] = peak
    index = stage()
    copy(m2_ref, r2_ref, core_peer, index, index).start()
    sent.append((r2_ref, index))
    landed(r2_ref, index)
    peak = jnp.maximum(peak, r2_ref[...])
    m3_ref[...] = peak
    last_maxima = stage()
    for j, o in enumerate(line):
        copy(m3_ref, r3_ref.at[j], line_peer[o], last_maxima, last_maxima).start()
    sent.append((r3_ref, last_maxima))

    signed = signed_ref[...]

    def rotate(slots_ref, out_ref, count):
        for k in range(count):
            cols = slice(k * HAD, (k + 1) * HAD)
            value = slots_ref[:, :, cols].reshape((here + 1) * pair, HAD)
            out_ref[:, :, cols] = dot(value, signed).reshape(here + 1, pair, HAD)

    landed(rbulka_ref.at[0:here], wave_a)
    wave_b = over_plane(bulkb_ref, rbulkb_ref)
    rotate(rbulka_ref, rota_ref, WA)
    landed(rbulkb_ref.at[0:here], wave_b)
    rotate(rbulkb_ref, rotb_ref, W - WA)

    landed(r3_ref, last_maxima)
    peak = jnp.maximum(peak, jnp.max(r3_ref[...], axis=0))

    scales = jnp.sqrt(peak + 1e-06)
    inverse = 0.0625 / scales
    z_at = lax.broadcasted_iota(jnp.int32, (NZ, LANES), 0)
    l_at = lax.broadcasted_iota(jnp.int32, (NZ, LANES), 1)
    core_send = stage()
    core_recv = [stage() for _ in range(W)]
    for k in range(W):
        cols = slice(k * HAD, (k + 1) * HAD)
        pick = l_at == z_at * stride + k
        factor = jnp.concatenate(
            [
                jnp.sum(
                    jnp.where(pick, jnp.broadcast_to(inverse[g : g + 1], (NZ, LANES)), 0.0),
                    axis=1,
                    keepdims=True,
                )
                for g in range(CORES)
            ],
            axis=0,
        )
        factor = jnp.broadcast_to(factor, (pair, HAD))
        total = jnp.zeros((pair, HAD), F32)
        rot_ref, at = (rota_ref, k) if k < WA else (rotb_ref, k - WA)
        for j in range(here + 1):
            value = rot_ref[j, :, at * HAD : (at + 1) * HAD] * factor
            value = jnp.clip(value, -clip_level, clip_level)
            total = total + value.astype(BF16).astype(F32)
        acc_ref[0, :, cols] = total[0:NZ]
        acc_ref[1, :, cols] = total[NZ:pair]
        copy(
            acc_ref.at[1 - c, :, cols], racc_ref.at[:, cols], core_peer, core_send, core_recv[k]
        ).start()
    sent.append((racc_ref, core_send))

    w_at = lax.broadcasted_iota(jnp.int32, (W, LANES), 0)
    k_at = lax.broadcasted_iota(jnp.int32, (W, LANES), 1)
    own = jnp.broadcast_to(jnp.where(c == 0, scales[0:1], scales[1:2]), (W, LANES))
    own_scale = jnp.sum(
        jnp.where(k_at == z * stride + w_at, own, 0.0), axis=1, keepdims=True
    )

    for k in range(W):
        landed(racc_ref.at[:, k * HAD : (k + 1) * HAD], core_recv[k])
        for h in range(2):
            cols = slice(k * HAD + h * LANES, k * HAD + (h + 1) * LANES)
            zs_ref[:, h * W + k, :] = acc_ref[c, :, cols] + racc_ref[:, cols]

    index = stage()
    for j, o in enumerate(line):
        copy(
            zs_ref.at[lax.rem(z + o, NZ)], rz_ref.at[j], line_peer[o], index, index
        ).start()
    sent.append((rz_ref, index))
    own_part = zs_ref[z]
    landed(rz_ref, index)
    total = own_part + jnp.sum(rz_ref[...], axis=0)

    wide = jnp.concatenate([total[0:W], total[W : 2 * W]], axis=1)
    parts = split_three(wide * own_scale)
    table = table_ref[...]
    gradient = (dot(parts[0], table) + dot(parts[1], table)) + dot(parts[2], table)
    gradient = gradient * 0.0625 * sign_row
    grad_ref[y] = gradient
    updated, _, _ = adam(gradient, adam_ref[0], adam_ref[1], adam_ref[2])
    updated = updated.astype(BF16).astype(F32)
    near_ref[len(near), 0:W] = updated[:, 0:LANES]
    near_ref[len(near), W : 2 * W] = updated[:, LANES:HAD]

    far_sem = stage()
    near_sem = stage()
    mine = near_ref.at[len(near)]
    slots = {o % NZ: (near_ref.at[i], near_sem) for i, o in enumerate(near)}
    slots.update({o % NZ: (far_ref.at[i], far_sem) for i, o in enumerate(far)})
    for o in line:
        slot, index = slots[o]
        copy(mine, slot, line_peer[o], index, index).start()
    sent.append((far_ref, far_sem))
    if near:
        sent.append((near_ref.at[0 : len(near)], near_sem))
    column_sem = stage()
    for o in column:
        copy(
            grad_ref.at[y], grad_ref.at[y], device(0, o, 0, 0), column_sem, column_sem
        ).start()
    sent.append((grad_ref.at[0 : NY - 1], column_sem))

    groups = []
    for j, o in enumerate(plane):
        if j and plane_hops(NX, NY, plane[j - 1]) == plane_hops(NX, NY, o):
            groups[-1][1] = j + 1
        else:
            groups.append([j, j + 1])
    core_sem = stage()

    def share(part, rows_ref):
        for k in range(W):
            both = jnp.concatenate([rows_ref[:, k, :], rows_ref[:, W + k, :]], axis=0)
            gb_ref[c, part, here, :, k * LANES : (k + 1) * LANES] = both.astype(BF16)
        send = stage()
        recv = {}
        for lo, hi in groups:
            index = stage()
            recv[lo] = index
            for j in range(lo, hi):
                copy(
                    gb_ref.at[c, part, here], gb_ref.at[c, part, j], plane_peer[j], send, index
                ).start()
        sent.append((gb_ref.at[c, part, 0:here], send))
        return recv

    def pass_on(part, recv):
        for lo, hi in reversed(groups):
            landed(gb_ref.at[c, part, lo:hi], recv[lo])
            hi = here + 1 if hi == here else hi
            piece = gb_ref.at[c, part, lo:hi]
            copy(piece, piece, core_peer, core_sem, core_sem).start()

    if near:
        landed(near_ref.at[0 : len(near)], near_sem)
    recv_near = share(0, near_ref)
    landed(far_ref, far_sem)
    recv_far = share(1, far_ref)
    pass_on(0, recv_near)
    pass_on(1, recv_far)
    landed(grad_ref.at[0 : NY - 1], column_sem)
    landed(gb_ref.at[1 - c], core_sem)
    sent.append((gb_ref.at[c], core_sem))

    for ref, index in sent:
        copy(ref, ref, core_peer, index, index).wait_send()


def write_kernel(
    sizes,
    gb_ref,
    grad_ref,
    master_ref,
    first_ref,
    second_ref,
    new_master_ref,
    new_first_ref,
    new_second_ref,
    out_ref,
    adam_ref,
):
    NX, NY, NZ, NB, W = sizes
    rows = NX * NZ * CORES
    plane = plane_offsets(NX, NY)
    slot_of = {o: j for j, o in enumerate(plane + [(0, 0)])}
    near, far = line_offsets(NZ)
    dp = lax.axis_index("dp")
    y = lax.axis_index("outer")
    z = lax.rem(dp // CORES, NZ)
    x = dp // (CORES * NZ)

    for at in range(NY):
        begin = piece_start(sizes, at)
        for k in range(W):
            lo = (begin + k) * HAD
            adam_ref[0, k : k + 1, :] = master_ref[0:1, lo : lo + HAD]
            adam_ref[1, k : k + 1, :] = first_ref[0:1, lo : lo + HAD]
            adam_ref[2, k : k + 1, :] = second_ref[0:1, lo : lo + HAD]
        results = adam(grad_ref[at], adam_ref[0], adam_ref[1], adam_ref[2])
        end = piece_start(sizes, at + 1) if at < NY - 1 else NB
        for k in range(end - begin):
            lo = (begin + k) * HAD
            for ref, value in zip((new_master_ref, new_first_ref, new_second_ref), results):
                ref[0:1, lo : lo + HAD] = value[k : k + 1, :]

    shape = (rows, CORES * 2 * NX * NZ)
    r_at = lax.broadcasted_iota(jnp.int32, shape, 0)
    g_at = lax.broadcasted_iota(jnp.int32, shape, 1)
    low = g_at % (NZ // 2)
    second_half = (g_at // (NZ // 2)) % 2
    ox = (g_at // NZ) % NX
    part = (g_at // (NZ * NX)) % 2
    core = g_at // (NZ * NX * 2)
    back = max(NZ // 4 - 1, 0)
    near_o = jnp.where(low == len(near), 0, low - back + (low >= back).astype(jnp.int32))
    oz = jnp.where(part == 0, near_o, low + NZ // 2 - back)
    source = (((x - ox + NX) % NX) * NZ + (z - oz + NZ) % NZ) * CORES + core
    pick = [
        ((r_at == source) & (second_half == h)).astype(F32).astype(BF16) for h in range(2)
    ]
    for oy in range(NY):
        at = lax.rem(y + NY - oy, NY)
        begin = piece_start(sizes, at) * HAD
        value = jnp.concatenate(
            [
                gb_ref[core, part, slot_of[(ox, oy)]]
                for core in range(CORES)
                for part in range(2)
                for ox in range(NX)
            ],
            axis=0,
        )
        tiles = [dot(pick[h], value).astype(BF16) for h in range(2)]
        for k in range(W):
            both = jnp.concatenate(
                [tile[:, k * LANES : (k + 1) * LANES] for tile in tiles], axis=1
            )
            cols = pl.ds(pl.multiple_of(begin + k * HAD, HAD), HAD)
            if k < W - 1:
                out_ref[:, cols] = both
            else:

                @pl.when((at == 0) | (at == NY - 1))
                def _():
                    out_ref[:, cols] = both


def build(mesh, NX, NZ, NB):
    NY = mesh.shape["outer"]
    W = -(-NB // NY)
    sizes = (NX, NY, NZ, NB, W)
    rows = NX * NZ * CORES
    pair = CORES * NZ
    n_plane = NX * NY - 1
    n_line = NZ - 1
    groups = len({plane_hops(NX, NY, o) for o in plane_offsets(NX, NY)})
    stages = 12 + W + 2 * (groups + 1)
    near, far = line_offsets(NZ)
    WA = (W + 1) // 2
    width = NB * HAD
    piece = W * HAD
    scratch = [
        pltpu.VMEM((rows, width), BF16),
        pltpu.VMEM((1, HAD), jnp.int32),
        pltpu.VMEM((3, 1, piece), F32),
        pltpu.VMEM((HAD, HAD), BF16),
        pltpu.VMEM((HAD, HAD), BF16),
        pltpu.VMEM((3, W, HAD), F32),
        pltpu.VMEM((NY, NX, pair, WA * HAD), BF16),
        pltpu.VMEM((NY, NX, pair, (W - WA) * HAD), BF16),
        pltpu.VMEM((n_plane + 1, pair, WA * HAD), BF16),
        pltpu.VMEM((n_plane + 1, pair, (W - WA) * HAD), BF16),
        pltpu.VMEM((n_plane + 1, pair, WA * HAD), F32),
        pltpu.VMEM((n_plane + 1, pair, (W - WA) * HAD), F32),
        pltpu.VMEM((NY, NX, CORES, LANES), F32),
        pltpu.VMEM((n_plane, CORES, LANES), F32),
        pltpu.VMEM((CORES, LANES), F32),
        pltpu.VMEM((CORES, LANES), F32),
        pltpu.VMEM((CORES, LANES), F32),
        pltpu.VMEM((n_line, CORES, LANES), F32),
        pltpu.VMEM((CORES, NZ, piece), F32),
        pltpu.VMEM((NZ, piece), F32),
        pltpu.VMEM((NZ, 2 * W, LANES), F32),
        pltpu.VMEM((n_line, 2 * W, LANES), F32),
        pltpu.VMEM((len(near) + 1, 2 * W, LANES), F32),
        pltpu.VMEM((len(far), 2 * W, LANES), F32),
        pltpu.SemaphoreType.DMA((5,)),
        pltpu.SemaphoreType.DMA((stages,)),
        pltpu.SemaphoreType.DMA((stages,)),
    ]
    vmem = pl.BlockSpec(memory_space=pltpu.VMEM)
    row = jax.ShapeDtypeStruct((1, width), F32)

    def per_device(replica_grads, hadamard_signs, master_rows, first_moment, second_moment):
        gathered, gradients = pl.pallas_call(
            functools.partial(exchange_kernel, sizes),
            out_shape=(
                pltpu.VMEM((CORES, 2, n_plane + 1, NZ, piece // 2), BF16),
                pltpu.VMEM((NY, W, HAD), F32),
            ),
            in_specs=[pl.BlockSpec(memory_space=pltpu.HBM)] * 5,
            out_specs=(vmem, vmem),
            scratch_shapes=scratch,
            compiler_params=pltpu.CompilerParams(
                collective_id=0, has_side_effects=True, vmem_limit_bytes=40 * 2**20
            ),
        )(
            *[
                pltpu.with_memory_space_constraint(array, pltpu.HBM)
                for array in (
                    replica_grads,
                    hadamard_signs.reshape(1, HAD),
                    master_rows,
                    first_moment,
                    second_moment,
                )
            ]
        )
        return pl.pallas_call(
            functools.partial(write_kernel, sizes),
            out_shape=(row, row, row, jax.ShapeDtypeStruct((rows, width), BF16)),
            in_specs=[vmem] * 5,
            out_specs=(vmem,) * 4,
            scratch_shapes=[pltpu.VMEM((3, W, HAD), F32)],
            compiler_params=pltpu.CompilerParams(vmem_limit_bytes=20 * 2**20),
        )(gathered, gradients, master_rows, first_moment, second_moment)

    in_specs = (P("dp", "outer", None, None), P(), P("dp", None), P("dp", None), P("dp", None))
    out_specs = (P("dp", None), P("dp", None), P("dp", None), P())
    return jax.shard_map(
        per_device, mesh=mesh, in_specs=in_specs, out_specs=out_specs, check_vma=False
    )


def solution(mesh):
    return build(mesh, 4, 16, 18)
```

```python
import functools

import jax
import jax.numpy as jnp
from jax import lax
from jax.experimental import pallas as pl
from jax.experimental.pallas import tpu as pltpu
from jax.sharding import PartitionSpec as P

HAD = 256
LANES = 128
STEP = 1000
CORES = 2

beta_one = 0.9
beta_two = 0.95
rate = 0.001
decay = 0.1
tiny_eps = 1e-08
clip_level = 1.5
first_fix = 1.0 - beta_one**STEP
second_fix = 1.0 - beta_two**STEP

F32 = jnp.float32
BF16 = jnp.bfloat16
MESH = pl.DeviceIdType.MESH


def ring_distance(offset, size):
    return min(offset, size - offset)


def hadamard(dtype):
    bits = lax.broadcasted_iota(jnp.int32, (HAD, HAD), 0) & lax.broadcasted_iota(
        jnp.int32, (HAD, HAD), 1
    )
    bits = bits ^ (bits >> 4)
    bits = bits ^ (bits >> 2)
    bits = bits ^ (bits >> 1)
    return (1 - 2 * (bits & 1)).astype(F32).astype(dtype)


def split_three(value):
    high = value.astype(BF16)
    rest = value - high.astype(F32)
    middle = rest.astype(BF16)
    low = (rest - middle.astype(F32)).astype(BF16)
    return high, middle, low


def dot(a, b):
    return jnp.dot(a, b, preferred_element_type=F32)


def adam(gradient, master, first, second):
    new_first = beta_one * first + (1.0 - beta_one) * gradient
    new_second = beta_two * second + (1.0 - beta_two) * gradient * gradient
    update = (
        new_first * (1.0 / first_fix) / (jnp.sqrt(new_second * (1.0 / second_fix)) + tiny_eps)
        + decay * master
    )
    return master - rate * update, new_first, new_second


def piece_start(sizes, at):
    NX, NY, NZ, NB, W = sizes
    return (at * (NB - W) + NY - 2) // (NY - 1)


def plane_offsets(NX, NY):
    plane = [(ox, oy) for oy in range(NY) for ox in range(NX) if ox or oy]
    return sorted(plane, key=lambda o: -plane_hops(NX, NY, o))


def plane_hops(NX, NY, o):
    return ring_distance(o[0], NX) + ring_distance(o[1], NY)


def line_offsets(NZ):
    back = max(NZ // 4 - 1, 0)
    near = [o for o in range(-back, NZ // 2 - back) if o]
    far = list(range(NZ // 2 - back, NZ - back))
    return near, far


def exchange_kernel(
    sizes,
    grads_hbm,
    signs_hbm,
    master_hbm,
    first_hbm,
    second_hbm,
    gb_ref,
    grad_ref,
    x_ref,
    signs_ref,
    state_ref,
    table_ref,
    signed_ref,
    adam_ref,
    bulk_ref,
    rbulk_ref,
    rot_ref,
    m1_ref,
    r1_ref,
    m2_ref,
    r2_ref,
    m3_ref,
    r3_ref,
    acc_ref,
    racc_ref,
    zs_ref,
    rz_ref,
    near_ref,
    far_ref,
    load_sems,
    send_sems,
    recv_sems,
):
    NX, NY, NZ, NB, W = sizes
    rows = NX * NZ * CORES
    pair = CORES * NZ
    stride = LANES // NZ

    dp = lax.axis_index("dp")
    y = lax.axis_index("outer")
    c = lax.rem(dp, CORES)
    z = lax.rem(dp // CORES, NZ)
    x = dp // (CORES * NZ)

    def first_block(at):
        return piece_start(sizes, at)

    def device(dx, dy, dz, dc):
        px = lax.rem(x + dx, NX)
        py = lax.rem(y + dy, NY)
        pz = lax.rem(z + dz, NZ)
        pc = lax.rem(c + dc, CORES)
        return ((px * NZ + pz) * CORES + pc, py)

    plane = plane_offsets(NX, NY)
    near, far = line_offsets(NZ)
    line = sorted([o % NZ for o in near + far], key=lambda o: -ring_distance(o, NZ))
    column = list(range(1, NY))
    core_peer = device(0, 0, 0, 1)
    plane_peer = [device(o[0], o[1], 0, 0) for o in plane]
    line_peer = {o: device(0, 0, o, 0) for o in line}
    here = len(plane)

    barrier = pltpu.get_barrier_semaphore()
    peers = [line_peer[o] for o in line] + plane_peer + [core_peer]
    for peer in peers:
        pl.semaphore_signal(barrier, inc=1, device_id=peer, device_id_type=MESH)

    begin = pl.multiple_of(first_block(y) * HAD, HAD)
    loads = [
        pltpu.make_async_copy(grads_hbm.at[0, 0], x_ref, load_sems.at[0]),
        pltpu.make_async_copy(signs_hbm, signs_ref, load_sems.at[1]),
    ]
    for i, hbm in enumerate((master_hbm, first_hbm, second_hbm)):
        loads.append(
            pltpu.make_async_copy(
                hbm.at[:, pl.ds(begin, W * HAD)], state_ref.at[i], load_sems.at[2 + i]
            )
        )
    for load in loads:
        load.start()

    counter = [0]
    sent = []

    def copy(src, dst, peer, send, recv):
        return pltpu.make_async_remote_copy(
            src_ref=src,
            dst_ref=dst,
            send_sem=send_sems.at[send],
            recv_sem=recv_sems.at[recv],
            device_id=peer,
            device_id_type=MESH,
        )

    def stage():
        counter[0] += 1
        return counter[0] - 1

    def landed(ref, index):
        copy(ref, ref, core_peer, index, index).wait_recv()

    p_at = lax.broadcasted_iota(jnp.int32, (rows, rows), 0)
    r_at = lax.broadcasted_iota(jnp.int32, (1, rows), 1)
    r_core = lax.rem(r_at, CORES)
    r_z = lax.rem(r_at // CORES, NZ)
    r_x = r_at // pair
    order = (p_at == r_x * pair + r_core * NZ + r_z).astype(F32).astype(BF16)

    table = hadamard(BF16)
    table_ref[...] = table

    loads[0].wait()

    lane = lax.rem(lax.broadcasted_iota(jnp.int32, (1, LANES), 1), stride)
    picks = [
        jnp.broadcast_to((lane == k).astype(F32), (HAD, LANES)).astype(BF16) for k in range(W)
    ]
    sums = [jnp.zeros((rows, LANES), F32) for _ in range(NY)]
    for block in range(NB):
        value = dot(order, x_ref[:, block * HAD : (block + 1) * HAD])
        square = value * value
        high = square.astype(BF16)
        low = (square - high.astype(F32)).astype(BF16)
        both = jnp.concatenate([high, low], axis=0)
        value = value.astype(BF16).reshape(NX, pair, HAD)
        for at in range(NY):
            k = block - first_block(at)
            if 0 <= k < W:
                part = dot(both, picks[k])
                sums[at] = sums[at] + (part[0:rows] + part[rows : 2 * rows])
                bulk_ref[k, at] = value
    row_at = lax.broadcasted_iota(jnp.int32, (rows, LANES), 0)
    lane_at = lax.broadcasted_iota(jnp.int32, (rows, LANES), 1)
    mine = row_at % NZ == lane_at // stride
    for at in range(NY):
        packed = jnp.where(mine, sums[at], 0.0).reshape(NX * CORES, NZ, LANES)
        packed = jnp.sum(packed, axis=1) * (1.0 / HAD)
        for px in range(NX):
            m1_ref[at, px] = packed[px * CORES : (px + 1) * CORES]

    pl.semaphore_wait(barrier, len(peers))

    def over_plane(parts_ref, slots_ref):
        index = stage()
        for j, o in enumerate(plane):
            piece = parts_ref.at[lax.rem(y + o[1], NY), lax.rem(x + o[0], NX)]
            copy(piece, slots_ref.at[j], plane_peer[j], index, index).start()
        sent.append((slots_ref.at[0:here], index))
        return index

    first_maxima = over_plane(m1_ref, r1_ref)
    ahead = 3
    waves = [over_plane(bulk_ref.at[k], rbulk_ref.at[k]) for k in range(min(ahead, W))]
    for k in range(W):
        rbulk_ref[k, here] = bulk_ref[k, y, x]

    diagonal = lax.broadcasted_iota(jnp.int32, (HAD, HAD), 0) == lax.broadcasted_iota(
        jnp.int32, (HAD, HAD), 1
    )
    for load in loads[1:]:
        load.wait()
    sign_row = signs_ref[...].astype(F32)
    signed_ref[...] = dot(
        jnp.where(diagonal, sign_row, 0.0).astype(BF16), table
    ).astype(BF16)
    for k in range(W):
        for i in range(3):
            adam_ref[i, k : k + 1, :] = state_ref[i, :, k * HAD : (k + 1) * HAD]

    landed(r1_ref, first_maxima)
    peak = jnp.maximum(m1_ref[y, x], jnp.max(r1_ref[...], axis=0))
    m2_ref[...] = peak
    index = stage()
    copy(m2_ref, r2_ref, core_peer, index, index).start()
    sent.append((r2_ref, index))
    landed(r2_ref, index)
    peak = jnp.maximum(peak, r2_ref[...])
    m3_ref[...] = peak
    last_maxima = stage()
    for j, o in enumerate(line):
        copy(m3_ref, r3_ref.at[j], line_peer[o], last_maxima, last_maxima).start()
    sent.append((r3_ref, last_maxima))

    signed = signed_ref[...]
    for k in range(W):
        landed(rbulk_ref.at[k, 0:here], waves[k])
        if k + ahead < W:
            waves.append(over_plane(bulk_ref.at[k + ahead], rbulk_ref.at[k + ahead]))
        value = rbulk_ref[k].reshape((here + 1) * pair, HAD)
        rot_ref[k] = dot(value, signed).reshape(here + 1, pair, HAD)

    landed(r3_ref, last_maxima)
    peak = jnp.maximum(peak, jnp.max(r3_ref[...], axis=0))

    scales = jnp.sqrt(peak + 1e-06)
    inverse = 0.0625 / scales
    z_at = lax.broadcasted_iota(jnp.int32, (NZ, LANES), 0)
    l_at = lax.broadcasted_iota(jnp.int32, (NZ, LANES), 1)
    core_send = stage()
    core_recv = [stage() for _ in range(W)]
    for k in range(W):
        cols = slice(k * HAD, (k + 1) * HAD)
        pick = l_at == z_at * stride + k
        factor = jnp.concatenate(
            [
                jnp.sum(
                    jnp.where(pick, jnp.broadcast_to(inverse[g : g + 1], (NZ, LANES)), 0.0),
                    axis=1,
                    keepdims=True,
                )
                for g in range(CORES)
            ],
            axis=0,
        )
        factor = jnp.broadcast_to(factor, (pair, HAD))
        total = jnp.zeros((pair, HAD), F32)
        for j in range(here + 1):
            value = jnp.clip(rot_ref[k, j] * factor, -clip_level, clip_level)
            total = total + value.astype(BF16).astype(F32)
        acc_ref[0, :, cols] = total[0:NZ]
        acc_ref[1, :, cols] = total[NZ:pair]
        copy(
            acc_ref.at[1 - c, :, cols], racc_ref.at[:, cols], core_peer, core_send, core_recv[k]
        ).start()
    sent.append((racc_ref, core_send))

    w_at = lax.broadcasted_iota(jnp.int32, (W, LANES), 0)
    k_at = lax.broadcasted_iota(jnp.int32, (W, LANES), 1)
    own = jnp.broadcast_to(jnp.where(c == 0, scales[0:1], scales[1:2]), (W, LANES))
    own_scale = jnp.sum(
        jnp.where(k_at == z * stride + w_at, own, 0.0), axis=1, keepdims=True
    )

    for k in range(W):
        landed(racc_ref.at[:, k * HAD : (k + 1) * HAD], core_recv[k])
        for h in range(2):
            cols = slice(k * HAD + h * LANES, k * HAD + (h + 1) * LANES)
            zs_ref[:, h * W + k, :] = acc_ref[c, :, cols] + racc_ref[:, cols]

    index = stage()
    for j, o in enumerate(line):
        copy(
            zs_ref.at[lax.rem(z + o, NZ)], rz_ref.at[j], line_peer[o], index, index
        ).start()
    sent.append((rz_ref, index))
    own_part = zs_ref[z]
    landed(rz_ref, index)
    total = own_part + jnp.sum(rz_ref[...], axis=0)

    wide = jnp.concatenate([total[0:W], total[W : 2 * W]], axis=1)
    parts = split_three(wide * own_scale)
    table = table_ref[...]
    gradient = (dot(parts[0], table) + dot(parts[1], table)) + dot(parts[2], table)
    gradient = gradient * 0.0625 * sign_row
    grad_ref[y] = gradient
    updated, _, _ = adam(gradient, adam_ref[0], adam_ref[1], adam_ref[2])
    updated = updated.astype(BF16).astype(F32)
    near_ref[len(near), 0:W] = updated[:, 0:LANES]
    near_ref[len(near), W : 2 * W] = updated[:, LANES:HAD]

    far_sem = stage()
    near_sem = stage()
    mine = near_ref.at[len(near)]
    slots = {o % NZ: (near_ref.at[i], near_sem) for i, o in enumerate(near)}
    slots.update({o % NZ: (far_ref.at[i], far_sem) for i, o in enumerate(far)})
    for o in line:
        slot, index = slots[o]
        copy(mine, slot, line_peer[o], index, index).start()
    sent.append((far_ref, far_sem))
    if near:
        sent.append((near_ref.at[0 : len(near)], near_sem))
    column_sem = stage()
    for o in column:
        copy(
            grad_ref.at[y], grad_ref.at[y], device(0, o, 0, 0), column_sem, column_sem
        ).start()
    sent.append((grad_ref.at[0 : NY - 1], column_sem))

    groups = []
    for j, o in enumerate(plane):
        if j and plane_hops(NX, NY, plane[j - 1]) == plane_hops(NX, NY, o):
            groups[-1][1] = j + 1
        else:
            groups.append([j, j + 1])
    core_sem = stage()

    def share(part, rows_ref):
        for k in range(W):
            both = jnp.concatenate([rows_ref[:, k, :], rows_ref[:, W + k, :]], axis=0)
            gb_ref[c, part, here, :, k * LANES : (k + 1) * LANES] = both.astype(BF16)
        send = stage()
        recv = {}
        for lo, hi in groups:
            index = stage()
            recv[lo] = index
            for j in range(lo, hi):
                copy(
                    gb_ref.at[c, part, here], gb_ref.at[c, part, j], plane_peer[j], send, index
                ).start()
        sent.append((gb_ref.at[c, part, 0:here], send))
        return recv

    def pass_on(part, recv):
        for lo, hi in reversed(groups):
            landed(gb_ref.at[c, part, lo:hi], recv[lo])
            hi = here + 1 if hi == here else hi
            piece = gb_ref.at[c, part, lo:hi]
            copy(piece, piece, core_peer, core_sem, core_sem).start()

    if near:
        landed(near_ref.at[0 : len(near)], near_sem)
    recv_near = share(0, near_ref)
    landed(far_ref, far_sem)
    recv_far = share(1, far_ref)
    pass_on(0, recv_near)
    pass_on(1, recv_far)
    landed(grad_ref.at[0 : NY - 1], column_sem)
    landed(gb_ref.at[1 - c], core_sem)
    sent.append((gb_ref.at[c], core_sem))

    for ref, index in sent:
        copy(ref, ref, core_peer, index, index).wait_send()


def write_kernel(
    sizes,
    gb_ref,
    grad_ref,
    master_ref,
    first_ref,
    second_ref,
    new_master_ref,
    new_first_ref,
    new_second_ref,
    out_ref,
    adam_ref,
):
    NX, NY, NZ, NB, W = sizes
    rows = NX * NZ * CORES
    plane = plane_offsets(NX, NY)
    slot_of = {o: j for j, o in enumerate(plane + [(0, 0)])}
    near, far = line_offsets(NZ)
    dp = lax.axis_index("dp")
    y = lax.axis_index("outer")
    z = lax.rem(dp // CORES, NZ)
    x = dp // (CORES * NZ)

    for at in range(NY):
        begin = piece_start(sizes, at)
        for k in range(W):
            lo = (begin + k) * HAD
            adam_ref[0, k : k + 1, :] = master_ref[0:1, lo : lo + HAD]
            adam_ref[1, k : k + 1, :] = first_ref[0:1, lo : lo + HAD]
            adam_ref[2, k : k + 1, :] = second_ref[0:1, lo : lo + HAD]
        results = adam(grad_ref[at], adam_ref[0], adam_ref[1], adam_ref[2])
        end = piece_start(sizes, at + 1) if at < NY - 1 else NB
        for k in range(end - begin):
            lo = (begin + k) * HAD
            for ref, value in zip((new_master_ref, new_first_ref, new_second_ref), results):
                ref[0:1, lo : lo + HAD] = value[k : k + 1, :]

    slots = CORES * 2 * NX * NZ
    r_at = lax.broadcasted_iota(jnp.int32, (rows, slots), 0)
    g_at = lax.broadcasted_iota(jnp.int32, (1, slots), 1)
    low = lax.rem(g_at, NZ // 2)
    second_half = lax.rem(g_at // (NZ // 2), 2)
    ox = lax.rem(g_at // NZ, NX)
    part = lax.rem(g_at // (NZ * NX), 2)
    core = g_at // (NZ * NX * 2)
    back = max(NZ // 4 - 1, 0)
    near_o = jnp.where(low == len(near), 0, low - back + (low >= back).astype(jnp.int32))
    oz = jnp.where(part == 0, near_o, low + NZ // 2 - back)
    source = (lax.rem(x - ox + NX, NX) * NZ + lax.rem(z - oz + NZ, NZ)) * CORES + core
    pick = [
        (r_at == jnp.where(second_half == h, source, -1)).astype(F32).astype(BF16)
        for h in range(2)
    ]
    for oy in range(NY):
        at = lax.rem(y + NY - oy, NY)
        begin = piece_start(sizes, at) * HAD
        value = jnp.concatenate(
            [
                gb_ref[core, part, slot_of[(ox, oy)]]
                for core in range(CORES)
                for part in range(2)
                for ox in range(NX)
            ],
            axis=0,
        )
        tiles = [dot(pick[h], value).astype(BF16) for h in range(2)]
        for k in range(W):
            both = jnp.concatenate(
                [tile[:, k * LANES : (k + 1) * LANES] for tile in tiles], axis=1
            )
            cols = pl.ds(pl.multiple_of(begin + k * HAD, HAD), HAD)
            if k < W - 1:
                out_ref[:, cols] = both
            else:

                @pl.when((at == 0) | (at == NY - 1))
                def _():
                    out_ref[:, cols] = both


def build(mesh, NX, NZ, NB):
    NY = mesh.shape["outer"]
    W = -(-NB // NY)
    sizes = (NX, NY, NZ, NB, W)
    rows = NX * NZ * CORES
    pair = CORES * NZ
    n_plane = NX * NY - 1
    n_line = NZ - 1
    groups = len({plane_hops(NX, NY, o) for o in plane_offsets(NX, NY)})
    stages = 10 + 2 * W + 2 * (groups + 1)
    near, far = line_offsets(NZ)
    width = NB * HAD
    piece = W * HAD
    scratch = [
        pltpu.VMEM((rows, width), BF16),
        pltpu.VMEM((1, HAD), jnp.int32),
        pltpu.VMEM((3, 1, piece), F32),
        pltpu.VMEM((HAD, HAD), BF16),
        pltpu.VMEM((HAD, HAD), BF16),
        pltpu.VMEM((3, W, HAD), F32),
        pltpu.VMEM((W, NY, NX, pair, HAD), BF16),
        pltpu.VMEM((W, n_plane + 1, pair, HAD), BF16),
        pltpu.VMEM((W, n_plane + 1, pair, HAD), F32),
        pltpu.VMEM((NY, NX, CORES, LANES), F32),
        pltpu.VMEM((n_plane, CORES, LANES), F32),
        pltpu.VMEM((CORES, LANES), F32),
        pltpu.VMEM((CORES, LANES), F32),
        pltpu.VMEM((CORES, LANES), F32),
        pltpu.VMEM((n_line, CORES, LANES), F32),
        pltpu.VMEM((CORES, NZ, piece), F32),
        pltpu.VMEM((NZ, piece), F32),
        pltpu.VMEM((NZ, 2 * W, LANES), F32),
        pltpu.VMEM((n_line, 2 * W, LANES), F32),
        pltpu.VMEM((len(near) + 1, 2 * W, LANES), F32),
        pltpu.VMEM((len(far), 2 * W, LANES), F32),
        pltpu.SemaphoreType.DMA((5,)),
        pltpu.SemaphoreType.DMA((stages,)),
        pltpu.SemaphoreType.DMA((stages,)),
    ]
    vmem = pl.BlockSpec(memory_space=pltpu.VMEM)
    row = jax.ShapeDtypeStruct((1, width), F32)

    def per_device(replica_grads, hadamard_signs, master_rows, first_moment, second_moment):
        gathered, gradients = pl.pallas_call(
            functools.partial(exchange_kernel, sizes),
            out_shape=(
                pltpu.VMEM((CORES, 2, n_plane + 1, NZ, piece // 2), BF16),
                pltpu.VMEM((NY, W, HAD), F32),
            ),
            in_specs=[pl.BlockSpec(memory_space=pltpu.HBM)] * 5,
            out_specs=(vmem, vmem),
            scratch_shapes=scratch,
            compiler_params=pltpu.CompilerParams(
                collective_id=0, has_side_effects=True, vmem_limit_bytes=40 * 2**20
            ),
        )(
            *[
                pltpu.with_memory_space_constraint(array, pltpu.HBM)
                for array in (
                    replica_grads,
                    hadamard_signs.reshape(1, HAD),
                    master_rows,
                    first_moment,
                    second_moment,
                )
            ]
        )
        return pl.pallas_call(
            functools.partial(write_kernel, sizes),
            out_shape=(row, row, row, jax.ShapeDtypeStruct((rows, width), BF16)),
            in_specs=[vmem] * 5,
            out_specs=(vmem,) * 4,
            scratch_shapes=[pltpu.VMEM((3, W, HAD), F32)],
            compiler_params=pltpu.CompilerParams(vmem_limit_bytes=20 * 2**20),
        )(gathered, gradients, master_rows, first_moment, second_moment)

    in_specs = (P("dp", "outer", None, None), P(), P("dp", None), P("dp", None), P("dp", None))
    out_specs = (P("dp", None), P("dp", None), P("dp", None), P())
    return jax.shard_map(
        per_device, mesh=mesh, in_specs=in_specs, out_specs=out_specs, check_vma=False
    )


def solution(mesh):
    return build(mesh, 4, 16, 18)
```

```python
import functools

import jax
import jax.numpy as jnp
from jax import lax
from jax.experimental import pallas as pl
from jax.experimental.pallas import tpu as pltpu
from jax.sharding import PartitionSpec as P

HAD = 256
LANES = 128
STEP = 1000
CORES = 2

beta_one = 0.9
beta_two = 0.95
rate = 0.001
decay = 0.1
tiny_eps = 1e-08
clip_level = 1.5
first_fix = 1.0 - beta_one**STEP
second_fix = 1.0 - beta_two**STEP

F32 = jnp.float32
BF16 = jnp.bfloat16
MESH = pl.DeviceIdType.MESH


def ring_distance(offset, size):
    return min(offset, size - offset)


def hadamard(dtype):
    bits = lax.broadcasted_iota(jnp.int32, (HAD, HAD), 0) & lax.broadcasted_iota(
        jnp.int32, (HAD, HAD), 1
    )
    bits = bits ^ (bits >> 4)
    bits = bits ^ (bits >> 2)
    bits = bits ^ (bits >> 1)
    return (1 - 2 * (bits & 1)).astype(F32).astype(dtype)


def split_three(value):
    high = value.astype(BF16)
    rest = value - high.astype(F32)
    middle = rest.astype(BF16)
    low = (rest - middle.astype(F32)).astype(BF16)
    return high, middle, low


def dot(a, b):
    return jnp.dot(a, b, preferred_element_type=F32)


def adam(gradient, master, first, second):
    new_first = beta_one * first + (1.0 - beta_one) * gradient
    new_second = beta_two * second + (1.0 - beta_two) * gradient * gradient
    update = (
        new_first * (1.0 / first_fix) / (jnp.sqrt(new_second * (1.0 / second_fix)) + tiny_eps)
        + decay * master
    )
    return master - rate * update, new_first, new_second


def piece_start(sizes, at):
    NX, NY, NZ, NB, W = sizes
    return (at * (NB - W) + NY - 2) // (NY - 1)


def plane_offsets(NX, NY):
    plane = [(ox, oy) for oy in range(NY) for ox in range(NX) if ox or oy]
    return sorted(plane, key=lambda o: -plane_hops(NX, NY, o))


def plane_hops(NX, NY, o):
    return ring_distance(o[0], NX) + ring_distance(o[1], NY)


def line_offsets(NZ):
    back = max(NZ // 4 - 1, 0)
    near = [o for o in range(-back, NZ // 2 - back) if o]
    far = list(range(NZ // 2 - back, NZ - back))
    return near, far


def exchange_kernel(
    sizes,
    grads_hbm,
    signs_hbm,
    master_hbm,
    first_hbm,
    second_hbm,
    gb_ref,
    grad_ref,
    x_ref,
    signs_ref,
    state_ref,
    table_ref,
    signed_ref,
    adam_ref,
    bulk_ref,
    rbulk_ref,
    rot_ref,
    m1_ref,
    r1_ref,
    m2_ref,
    r2_ref,
    m3_ref,
    r3_ref,
    acc_ref,
    racc_ref,
    zs_ref,
    rz_ref,
    near_ref,
    far_ref,
    load_sems,
    send_sems,
    recv_sems,
):
    NX, NY, NZ, NB, W = sizes
    rows = NX * NZ * CORES
    pair = CORES * NZ
    stride = LANES // NZ

    dp = lax.axis_index("dp")
    y = lax.axis_index("outer")
    c = lax.rem(dp, CORES)
    z = lax.rem(dp // CORES, NZ)
    x = dp // (CORES * NZ)

    def first_block(at):
        return piece_start(sizes, at)

    def device(dx, dy, dz, dc):
        px = lax.rem(x + dx, NX)
        py = lax.rem(y + dy, NY)
        pz = lax.rem(z + dz, NZ)
        pc = lax.rem(c + dc, CORES)
        return ((px * NZ + pz) * CORES + pc, py)

    plane = plane_offsets(NX, NY)
    near, far = line_offsets(NZ)
    line = sorted([o % NZ for o in near + far], key=lambda o: -ring_distance(o, NZ))
    column = list(range(1, NY))
    core_peer = device(0, 0, 0, 1)
    plane_peer = [device(o[0], o[1], 0, 0) for o in plane]
    line_peer = {o: device(0, 0, o, 0) for o in line}
    here = len(plane)

    barrier = pltpu.get_barrier_semaphore()
    peers = [line_peer[o] for o in line] + plane_peer + [core_peer]
    for peer in peers:
        pl.semaphore_signal(barrier, inc=1, device_id=peer, device_id_type=MESH)

    begin = pl.multiple_of(first_block(y) * HAD, HAD)
    loads = [
        pltpu.make_async_copy(grads_hbm.at[0, 0], x_ref, load_sems.at[0]),
        pltpu.make_async_copy(signs_hbm, signs_ref, load_sems.at[1]),
    ]
    for i, hbm in enumerate((master_hbm, first_hbm, second_hbm)):
        loads.append(
            pltpu.make_async_copy(
                hbm.at[:, pl.ds(begin, W * HAD)], state_ref.at[i], load_sems.at[2 + i]
            )
        )
    for load in loads:
        load.start()

    counter = [0]
    sent = []

    def copy(src, dst, peer, send, recv):
        return pltpu.make_async_remote_copy(
            src_ref=src,
            dst_ref=dst,
            send_sem=send_sems.at[send],
            recv_sem=recv_sems.at[recv],
            device_id=peer,
            device_id_type=MESH,
        )

    def stage():
        counter[0] += 1
        return counter[0] - 1

    def landed(ref, index):
        copy(ref, ref, core_peer, index, index).wait_recv()

    p_at = lax.broadcasted_iota(jnp.int32, (rows, rows), 0)
    r_at = lax.broadcasted_iota(jnp.int32, (1, rows), 1)
    r_core = lax.rem(r_at, CORES)
    r_z = lax.rem(r_at // CORES, NZ)
    r_x = r_at // pair
    order = (p_at == r_x * pair + r_core * NZ + r_z).astype(F32).astype(BF16)

    table = hadamard(BF16)
    table_ref[...] = table

    loads[0].wait()

    lane = lax.rem(lax.broadcasted_iota(jnp.int32, (1, LANES), 1), stride)
    picks = [
        jnp.broadcast_to((lane == k).astype(F32), (HAD, LANES)).astype(BF16) for k in range(W)
    ]
    sums = [jnp.zeros((rows, LANES), F32) for _ in range(NY)]
    for block in range(NB):
        value = dot(order, x_ref[:, block * HAD : (block + 1) * HAD])
        square = value * value
        high = square.astype(BF16)
        low = (square - high.astype(F32)).astype(BF16)
        both = jnp.concatenate([high, low], axis=0)
        value = value.astype(BF16).reshape(NX, pair, HAD)
        for at in range(NY):
            k = block - first_block(at)
            if 0 <= k < W:
                part = dot(both, picks[k])
                sums[at] = sums[at] + (part[0:rows] + part[rows : 2 * rows])
                bulk_ref[k, at] = value
    row_at = lax.broadcasted_iota(jnp.int32, (rows, LANES), 0)
    lane_at = lax.broadcasted_iota(jnp.int32, (rows, LANES), 1)
    mine = row_at % NZ == lane_at // stride
    for at in range(NY):
        packed = jnp.where(mine, sums[at], 0.0).reshape(NX * CORES, NZ, LANES)
        packed = jnp.sum(packed, axis=1) * (1.0 / HAD)
        for px in range(NX):
            m1_ref[at, px] = packed[px * CORES : (px + 1) * CORES]

    pl.semaphore_wait(barrier, len(peers))

    def over_plane(parts_ref, slots_ref):
        index = stage()
        for j, o in enumerate(plane):
            piece = parts_ref.at[lax.rem(y + o[1], NY), lax.rem(x + o[0], NX)]
            copy(piece, slots_ref.at[j], plane_peer[j], index, index).start()
        sent.append((slots_ref.at[0:here], index))
        return index

    first_maxima = over_plane(m1_ref, r1_ref)
    ahead = 3
    waves = [over_plane(bulk_ref.at[k], rbulk_ref.at[k]) for k in range(ahead - 1)]
    for k in range(W):
        rbulk_ref[k, here] = bulk_ref[k, y, x]

    diagonal = lax.broadcasted_iota(jnp.int32, (HAD, HAD), 0) == lax.broadcasted_iota(
        jnp.int32, (HAD, HAD), 1
    )
    for load in loads[1:]:
        load.wait()
    sign_row = signs_ref[...].astype(F32)
    signed_ref[...] = dot(
        jnp.where(diagonal, sign_row, 0.0).astype(BF16), table
    ).astype(BF16)
    for k in range(W):
        for i in range(3):
            adam_ref[i, k : k + 1, :] = state_ref[i, :, k * HAD : (k + 1) * HAD]

    landed(r1_ref, first_maxima)
    waves.append(over_plane(bulk_ref.at[ahead - 1], rbulk_ref.at[ahead - 1]))
    peak = jnp.maximum(m1_ref[y, x], jnp.max(r1_ref[...], axis=0))
    m2_ref[...] = peak
    index = stage()
    copy(m2_ref, r2_ref, core_peer, index, index).start()
    sent.append((r2_ref, index))
    landed(r2_ref, index)
    peak = jnp.maximum(peak, r2_ref[...])
    m3_ref[...] = peak
    last_maxima = stage()
    for j, o in enumerate(line):
        copy(m3_ref, r3_ref.at[j], line_peer[o], last_maxima, last_maxima).start()
    sent.append((r3_ref, last_maxima))

    signed = signed_ref[...]
    for k in range(W):
        landed(rbulk_ref.at[k, 0:here], waves[k])
        if k + ahead < W:
            waves.append(over_plane(bulk_ref.at[k + ahead], rbulk_ref.at[k + ahead]))
        value = rbulk_ref[k].reshape((here + 1) * pair, HAD)
        rot_ref[k] = dot(value, signed).reshape(here + 1, pair, HAD)

    landed(r3_ref, last_maxima)
    peak = jnp.maximum(peak, jnp.max(r3_ref[...], axis=0))

    scales = jnp.sqrt(peak + 1e-06)
    inverse = 0.0625 / scales
    z_at = lax.broadcasted_iota(jnp.int32, (NZ, LANES), 0)
    l_at = lax.broadcasted_iota(jnp.int32, (NZ, LANES), 1)
    core_send = stage()
    core_recv = [stage() for _ in range(W)]
    for k in range(W):
        cols = slice(k * HAD, (k + 1) * HAD)
        pick = l_at == z_at * stride + k
        factor = jnp.concatenate(
            [
                jnp.sum(
                    jnp.where(pick, jnp.broadcast_to(inverse[g : g + 1], (NZ, LANES)), 0.0),
                    axis=1,
                    keepdims=True,
                )
                for g in range(CORES)
            ],
            axis=0,
        )
        factor = jnp.broadcast_to(factor, (pair, HAD))
        total = jnp.zeros((pair, HAD), F32)
        for j in range(here + 1):
            value = jnp.clip(rot_ref[k, j] * factor, -clip_level, clip_level)
            total = total + value.astype(BF16).astype(F32)
        acc_ref[0, :, cols] = total[0:NZ]
        acc_ref[1, :, cols] = total[NZ:pair]
        copy(
            acc_ref.at[1 - c, :, cols], racc_ref.at[:, cols], core_peer, core_send, core_recv[k]
        ).start()
    sent.append((racc_ref, core_send))

    w_at = lax.broadcasted_iota(jnp.int32, (W, LANES), 0)
    k_at = lax.broadcasted_iota(jnp.int32, (W, LANES), 1)
    own = jnp.broadcast_to(jnp.where(c == 0, scales[0:1], scales[1:2]), (W, LANES))
    own_scale = jnp.sum(
        jnp.where(k_at == z * stride + w_at, own, 0.0), axis=1, keepdims=True
    )

    for k in range(W):
        landed(racc_ref.at[:, k * HAD : (k + 1) * HAD], core_recv[k])
        for h in range(2):
            cols = slice(k * HAD + h * LANES, k * HAD + (h + 1) * LANES)
            zs_ref[:, h * W + k, :] = acc_ref[c, :, cols] + racc_ref[:, cols]

    index = stage()
    for j, o in enumerate(line):
        copy(
            zs_ref.at[lax.rem(z + o, NZ)], rz_ref.at[j], line_peer[o], index, index
        ).start()
    sent.append((rz_ref, index))
    own_part = zs_ref[z]
    landed(rz_ref, index)
    total = own_part + jnp.sum(rz_ref[...], axis=0)

    wide = jnp.concatenate([total[0:W], total[W : 2 * W]], axis=1)
    parts = split_three(wide * own_scale)
    table = table_ref[...]
    gradient = (dot(parts[0], table) + dot(parts[1], table)) + dot(parts[2], table)
    gradient = gradient * 0.0625 * sign_row
    grad_ref[y] = gradient
    updated, _, _ = adam(gradient, adam_ref[0], adam_ref[1], adam_ref[2])
    updated = updated.astype(BF16).astype(F32)
    near_ref[len(near), 0:W] = updated[:, 0:LANES]
    near_ref[len(near), W : 2 * W] = updated[:, LANES:HAD]

    far_sem = stage()
    near_sem = stage()
    mine = near_ref.at[len(near)]
    slots = {o % NZ: (near_ref.at[i], near_sem) for i, o in enumerate(near)}
    slots.update({o % NZ: (far_ref.at[i], far_sem) for i, o in enumerate(far)})
    for o in line:
        slot, index = slots[o]
        copy(mine, slot, line_peer[o], index, index).start()
    sent.append((far_ref, far_sem))
    if near:
        sent.append((near_ref.at[0 : len(near)], near_sem))
    column_sem = stage()
    for o in column:
        copy(
            grad_ref.at[y], grad_ref.at[y], device(0, o, 0, 0), column_sem, column_sem
        ).start()
    sent.append((grad_ref.at[0 : NY - 1], column_sem))

    core_sem = stage()
    gathered = (gb_ref.at[c, 0], gb_ref.at[c, 1])

    def pack(part, rows_ref):
        for k in range(W):
            both = jnp.concatenate([rows_ref[:, k, :], rows_ref[:, W + k, :]], axis=0)
            gb_ref[c, part, 0, :, k * LANES : (k + 1) * LANES] = both.astype(BF16)

    def along(part, axis, count):
        slots_ref = gathered[part]
        extent = (NX, NY)[axis]
        send = stage()
        recv = {}
        for o in sorted(range(1, extent), key=lambda o: -ring_distance(o, extent)):
            recv[o] = stage()
            peer = device(o, 0, 0, 0) if axis == 0 else device(0, o, 0, 0)
            copy(
                slots_ref.at[0:count],
                slots_ref.at[count * o : count * (o + 1)],
                peer,
                send,
                recv[o],
            ).start()
        sent.append((slots_ref.at[count : count * extent], send))
        return recv

    def arrive(part, recv, count, forward):
        slots_ref = gathered[part]
        for o in sorted(recv, key=lambda o: ring_distance(o, len(recv) + 1)):
            piece = slots_ref.at[count * o : count * (o + 1)]
            landed(piece, recv[o])
            if forward:
                copy(piece, piece, core_peer, core_sem, core_sem).start()

    def pass_on(part, count):
        piece = gathered[part].at[0:count]
        copy(piece, piece, core_peer, core_sem, core_sem).start()

    if near:
        landed(near_ref.at[0 : len(near)], near_sem)
    pack(0, near_ref)
    near_x = along(0, 0, 1)
    landed(far_ref, far_sem)
    pack(1, far_ref)
    far_y = along(1, 1, 1)
    arrive(0, near_x, 1, False)
    near_y = along(0, 1, NX)
    pass_on(0, NX)
    arrive(1, far_y, 1, False)
    far_x = along(1, 0, NY)
    pass_on(1, NY)
    arrive(0, near_y, NX, True)
    arrive(1, far_x, NY, True)
    landed(grad_ref.at[0 : NY - 1], column_sem)
    landed(gb_ref.at[1 - c], core_sem)
    sent.append((gb_ref.at[c], core_sem))

    for ref, index in sent:
        copy(ref, ref, core_peer, index, index).wait_send()


def write_kernel(
    sizes,
    gb_ref,
    grad_ref,
    master_ref,
    first_ref,
    second_ref,
    new_master_ref,
    new_first_ref,
    new_second_ref,
    out_ref,
    adam_ref,
):
    NX, NY, NZ, NB, W = sizes
    rows = NX * NZ * CORES
    near, far = line_offsets(NZ)
    dp = lax.axis_index("dp")
    y = lax.axis_index("outer")
    z = lax.rem(dp // CORES, NZ)
    x = dp // (CORES * NZ)

    for at in range(NY):
        begin = piece_start(sizes, at)
        for k in range(W):
            lo = (begin + k) * HAD
            adam_ref[0, k : k + 1, :] = master_ref[0:1, lo : lo + HAD]
            adam_ref[1, k : k + 1, :] = first_ref[0:1, lo : lo + HAD]
            adam_ref[2, k : k + 1, :] = second_ref[0:1, lo : lo + HAD]
        results = adam(grad_ref[at], adam_ref[0], adam_ref[1], adam_ref[2])
        end = piece_start(sizes, at + 1) if at < NY - 1 else NB
        for k in range(end - begin):
            lo = (begin + k) * HAD
            for ref, value in zip((new_master_ref, new_first_ref, new_second_ref), results):
                ref[0:1, lo : lo + HAD] = value[k : k + 1, :]

    slots = rows
    deep = NZ // 2
    r_at = lax.broadcasted_iota(jnp.int32, (rows, slots), 0)
    g_at = lax.broadcasted_iota(jnp.int32, (1, slots), 1)
    low = lax.rem(g_at, deep)
    ox = lax.rem(g_at // deep, NX)
    part = lax.rem(g_at // (deep * NX), 2)
    core = g_at // (deep * NX * 2)
    back = max(NZ // 4 - 1, 0)
    near_o = jnp.where(low == len(near), 0, low - back + (low >= back).astype(jnp.int32))
    oz = jnp.where(part == 0, near_o, low + NZ // 2 - back)
    source = (lax.rem(x - ox + NX, NX) * NZ + lax.rem(z - oz + NZ, NZ)) * CORES + core
    pick = (r_at == source).astype(F32).astype(BF16)
    for oy in range(NY):
        at = lax.rem(y + NY - oy, NY)
        begin = piece_start(sizes, at) * HAD
        tiles = []
        for h in range(2):
            value = jnp.concatenate(
                [
                    gb_ref[
                        core, part, ox * NY + oy if part else oy * NX + ox, h * deep : (h + 1) * deep
                    ]
                    for core in range(CORES)
                    for part in range(2)
                    for ox in range(NX)
                ],
                axis=0,
            )
            tiles.append(dot(pick, value).astype(BF16))
        for k in range(W):
            both = jnp.concatenate(
                [tile[:, k * LANES : (k + 1) * LANES] for tile in tiles], axis=1
            )
            cols = pl.ds(pl.multiple_of(begin + k * HAD, HAD), HAD)
            if k < W - 1:
                out_ref[:, cols] = both
            else:

                @pl.when((at == 0) | (at == NY - 1))
                def _():
                    out_ref[:, cols] = both


def build(mesh, NX, NZ, NB):
    NY = mesh.shape["outer"]
    W = -(-NB // NY)
    sizes = (NX, NY, NZ, NB, W)
    rows = NX * NZ * CORES
    pair = CORES * NZ
    n_plane = NX * NY - 1
    n_line = NZ - 1
    stages = 10 + 2 * W + 2 * (NX + NY)
    near, far = line_offsets(NZ)
    width = NB * HAD
    piece = W * HAD
    scratch = [
        pltpu.VMEM((rows, width), BF16),
        pltpu.VMEM((1, HAD), jnp.int32),
        pltpu.VMEM((3, 1, piece), F32),
        pltpu.VMEM((HAD, HAD), BF16),
        pltpu.VMEM((HAD, HAD), BF16),
        pltpu.VMEM((3, W, HAD), F32),
        pltpu.VMEM((W, NY, NX, pair, HAD), BF16),
        pltpu.VMEM((W, n_plane + 1, pair, HAD), BF16),
        pltpu.VMEM((W, n_plane + 1, pair, HAD), F32),
        pltpu.VMEM((NY, NX, CORES, LANES), F32),
        pltpu.VMEM((n_plane, CORES, LANES), F32),
        pltpu.VMEM((CORES, LANES), F32),
        pltpu.VMEM((CORES, LANES), F32),
        pltpu.VMEM((CORES, LANES), F32),
        pltpu.VMEM((n_line, CORES, LANES), F32),
        pltpu.VMEM((CORES, NZ, piece), F32),
        pltpu.VMEM((NZ, piece), F32),
        pltpu.VMEM((NZ, 2 * W, LANES), F32),
        pltpu.VMEM((n_line, 2 * W, LANES), F32),
        pltpu.VMEM((len(near) + 1, 2 * W, LANES), F32),
        pltpu.VMEM((len(far), 2 * W, LANES), F32),
        pltpu.SemaphoreType.DMA((5,)),
        pltpu.SemaphoreType.DMA((stages,)),
        pltpu.SemaphoreType.DMA((stages,)),
    ]
    vmem = pl.BlockSpec(memory_space=pltpu.VMEM)
    row = jax.ShapeDtypeStruct((1, width), F32)

    def per_device(replica_grads, hadamard_signs, master_rows, first_moment, second_moment):
        gathered, gradients = pl.pallas_call(
            functools.partial(exchange_kernel, sizes),
            out_shape=(
                pltpu.VMEM((CORES, 2, n_plane + 1, NZ, piece // 2), BF16),
                pltpu.VMEM((NY, W, HAD), F32),
            ),
            in_specs=[pl.BlockSpec(memory_space=pltpu.HBM)] * 5,
            out_specs=(vmem, vmem),
            scratch_shapes=scratch,
            compiler_params=pltpu.CompilerParams(
                collective_id=0, has_side_effects=True, vmem_limit_bytes=40 * 2**20
            ),
        )(
            *[
                pltpu.with_memory_space_constraint(array, pltpu.HBM)
                for array in (
                    replica_grads,
                    hadamard_signs.reshape(1, HAD),
                    master_rows,
                    first_moment,
                    second_moment,
                )
            ]
        )
        return pl.pallas_call(
            functools.partial(write_kernel, sizes),
            out_shape=(row, row, row, jax.ShapeDtypeStruct((rows, width), BF16)),
            in_specs=[vmem] * 5,
            out_specs=(vmem,) * 4,
            scratch_shapes=[pltpu.VMEM((3, W, HAD), F32)],
            compiler_params=pltpu.CompilerParams(vmem_limit_bytes=20 * 2**20),
        )(gathered, gradients, master_rows, first_moment, second_moment)

    in_specs = (P("dp", "outer", None, None), P(), P("dp", None), P("dp", None), P("dp", None))
    out_specs = (P("dp", None), P("dp", None), P("dp", None), P())
    return jax.shard_map(
        per_device, mesh=mesh, in_specs=in_specs, out_specs=out_specs, check_vma=False
    )


def solution(mesh):
    return build(mesh, 4, 16, 18)
```

```python
import functools

import jax
import jax.numpy as jnp
from jax import lax
from jax.experimental import pallas as pl
from jax.experimental.pallas import tpu as pltpu
from jax.sharding import PartitionSpec as P

HAD = 256
LANES = 128
STEP = 1000
CORES = 2

beta_one = 0.9
beta_two = 0.95
rate = 0.001
decay = 0.1
tiny_eps = 1e-08
clip_level = 1.5
first_fix = 1.0 - beta_one**STEP
second_fix = 1.0 - beta_two**STEP

F32 = jnp.float32
BF16 = jnp.bfloat16
MESH = pl.DeviceIdType.MESH


def ring_distance(offset, size):
    return min(offset, size - offset)


def hadamard(dtype):
    bits = lax.broadcasted_iota(jnp.int32, (HAD, HAD), 0) & lax.broadcasted_iota(
        jnp.int32, (HAD, HAD), 1
    )
    bits = bits ^ (bits >> 4)
    bits = bits ^ (bits >> 2)
    bits = bits ^ (bits >> 1)
    return (1 - 2 * (bits & 1)).astype(F32).astype(dtype)


def split_three(value):
    high = value.astype(BF16)
    rest = value - high.astype(F32)
    middle = rest.astype(BF16)
    low = (rest - middle.astype(F32)).astype(BF16)
    return high, middle, low


def dot(a, b):
    return jnp.dot(a, b, preferred_element_type=F32)


def adam(gradient, master, first, second):
    new_first = beta_one * first + (1.0 - beta_one) * gradient
    new_second = beta_two * second + (1.0 - beta_two) * gradient * gradient
    update = (
        new_first * (1.0 / first_fix) / (jnp.sqrt(new_second * (1.0 / second_fix)) + tiny_eps)
        + decay * master
    )
    return master - rate * update, new_first, new_second


def piece_start(sizes, at):
    NX, NY, NZ, NB, W = sizes
    return (at * (NB - W) + NY - 2) // (NY - 1)


def plane_offsets(NX, NY):
    plane = [(ox, oy) for oy in range(NY) for ox in range(NX) if ox or oy]
    return sorted(plane, key=lambda o: -plane_hops(NX, NY, o))


def plane_hops(NX, NY, o):
    return ring_distance(o[0], NX) + ring_distance(o[1], NY)


def line_offsets(NZ):
    back = max(NZ // 4 - 1, 0)
    near = [o for o in range(-back, NZ // 2 - back) if o]
    far = list(range(NZ // 2 - back, NZ - back))
    return near, far


def exchange_kernel(
    sizes,
    grads_hbm,
    signs_hbm,
    master_hbm,
    first_hbm,
    second_hbm,
    ga_ref,
    gb_ref,
    grad_ref,
    x_ref,
    signs_ref,
    state_ref,
    table_ref,
    signed_ref,
    adam_ref,
    bulk_ref,
    rbulk_ref,
    rot_ref,
    m1_ref,
    r1_ref,
    m2_ref,
    r2_ref,
    m3_ref,
    r3_ref,
    acc_ref,
    racc_ref,
    zs_ref,
    rz_ref,
    near_ref,
    far_ref,
    load_sems,
    send_sems,
    recv_sems,
):
    NX, NY, NZ, NB, W = sizes
    rows = NX * NZ * CORES
    pair = CORES * NZ
    stride = LANES // NZ

    dp = lax.axis_index("dp")
    y = lax.axis_index("outer")
    c = lax.rem(dp, CORES)
    z = lax.rem(dp // CORES, NZ)
    x = dp // (CORES * NZ)

    def first_block(at):
        return piece_start(sizes, at)

    def device(dx, dy, dz, dc):
        px = lax.rem(x + dx, NX)
        py = lax.rem(y + dy, NY)
        pz = lax.rem(z + dz, NZ)
        pc = lax.rem(c + dc, CORES)
        return ((px * NZ + pz) * CORES + pc, py)

    plane = plane_offsets(NX, NY)
    near, far = line_offsets(NZ)
    line = sorted([o % NZ for o in near + far], key=lambda o: -ring_distance(o, NZ))
    column = list(range(1, NY))
    core_peer = device(0, 0, 0, 1)
    plane_peer = [device(o[0], o[1], 0, 0) for o in plane]
    line_peer = {o: device(0, 0, o, 0) for o in line}
    here = len(plane)

    barrier = pltpu.get_barrier_semaphore()
    peers = [line_peer[o] for o in line] + plane_peer + [core_peer]
    for peer in peers:
        pl.semaphore_signal(barrier, inc=1, device_id=peer, device_id_type=MESH)

    begin = pl.multiple_of(first_block(y) * HAD, HAD)
    loads = [
        pltpu.make_async_copy(grads_hbm.at[0, 0], x_ref, load_sems.at[0]),
        pltpu.make_async_copy(signs_hbm, signs_ref, load_sems.at[1]),
    ]
    for i, hbm in enumerate((master_hbm, first_hbm, second_hbm)):
        loads.append(
            pltpu.make_async_copy(
                hbm.at[:, pl.ds(begin, W * HAD)], state_ref.at[i], load_sems.at[2 + i]
            )
        )
    for load in loads:
        load.start()

    counter = [0]
    sent = []

    def copy(src, dst, peer, send, recv):
        return pltpu.make_async_remote_copy(
            src_ref=src,
            dst_ref=dst,
            send_sem=send_sems.at[send],
            recv_sem=recv_sems.at[recv],
            device_id=peer,
            device_id_type=MESH,
        )

    def stage():
        counter[0] += 1
        return counter[0] - 1

    def landed(ref, index):
        copy(ref, ref, core_peer, index, index).wait_recv()

    p_at = lax.broadcasted_iota(jnp.int32, (rows, rows), 0)
    r_at = lax.broadcasted_iota(jnp.int32, (1, rows), 1)
    r_core = lax.rem(r_at, CORES)
    r_z = lax.rem(r_at // CORES, NZ)
    r_x = r_at // pair
    order = (p_at == r_x * pair + r_core * NZ + r_z).astype(F32).astype(BF16)

    table = hadamard(BF16)
    table_ref[...] = table

    loads[0].wait()

    lane = lax.rem(lax.broadcasted_iota(jnp.int32, (1, LANES), 1), stride)
    picks = [
        jnp.broadcast_to((lane == k).astype(F32), (HAD, LANES)).astype(BF16) for k in range(W)
    ]
    sums = [jnp.zeros((rows, LANES), F32) for _ in range(NY)]
    for block in range(NB):
        value = dot(order, x_ref[:, block * HAD : (block + 1) * HAD])
        square = value * value
        high = square.astype(BF16)
        low = (square - high.astype(F32)).astype(BF16)
        both = jnp.concatenate([high, low], axis=0)
        value = value.astype(BF16).reshape(NX, pair, HAD)
        for at in range(NY):
            k = block - first_block(at)
            if 0 <= k < W:
                part = dot(both, picks[k])
                sums[at] = sums[at] + (part[0:rows] + part[rows : 2 * rows])
                bulk_ref[k, at] = value
    row_at = lax.broadcasted_iota(jnp.int32, (rows, LANES), 0)
    lane_at = lax.broadcasted_iota(jnp.int32, (rows, LANES), 1)
    mine = row_at % NZ == lane_at // stride
    for at in range(NY):
        packed = jnp.where(mine, sums[at], 0.0).reshape(NX * CORES, NZ, LANES)
        packed = jnp.sum(packed, axis=1) * (1.0 / HAD)
        for px in range(NX):
            m1_ref[at, px] = packed[px * CORES : (px + 1) * CORES]

    pl.semaphore_wait(barrier, len(peers))

    def over_plane(parts_ref, slots_ref):
        index = stage()
        for j, o in enumerate(plane):
            piece = parts_ref.at[lax.rem(y + o[1], NY), lax.rem(x + o[0], NX)]
            copy(piece, slots_ref.at[j], plane_peer[j], index, index).start()
        sent.append((slots_ref.at[0:here], index))
        return index

    first_maxima = over_plane(m1_ref, r1_ref)
    ahead = 3
    waves = [over_plane(bulk_ref.at[k], rbulk_ref.at[k]) for k in range(ahead - 1)]
    for k in range(W):
        rbulk_ref[k, here] = bulk_ref[k, y, x]

    diagonal = lax.broadcasted_iota(jnp.int32, (HAD, HAD), 0) == lax.broadcasted_iota(
        jnp.int32, (HAD, HAD), 1
    )
    for load in loads[1:]:
        load.wait()
    sign_row = signs_ref[...].astype(F32)
    signed_ref[...] = dot(
        jnp.where(diagonal, sign_row, 0.0).astype(BF16), table
    ).astype(BF16)
    for k in range(W):
        for i in range(3):
            adam_ref[i, k : k + 1, :] = state_ref[i, :, k * HAD : (k + 1) * HAD]

    landed(r1_ref, first_maxima)
    waves.append(over_plane(bulk_ref.at[ahead - 1], rbulk_ref.at[ahead - 1]))
    peak = jnp.maximum(m1_ref[y, x], jnp.max(r1_ref[...], axis=0))
    m2_ref[...] = peak
    index = stage()
    copy(m2_ref, r2_ref, core_peer, index, index).start()
    sent.append((r2_ref, index))
    landed(r2_ref, index)
    peak = jnp.maximum(peak, r2_ref[...])
    m3_ref[...] = peak
    last_maxima = stage()
    for j, o in enumerate(line):
        copy(m3_ref, r3_ref.at[j], line_peer[o], last_maxima, last_maxima).start()
    sent.append((r3_ref, last_maxima))

    signed = signed_ref[...]
    for k in range(W):
        landed(rbulk_ref.at[k, 0:here], waves[k])
        if k + ahead < W:
            waves.append(over_plane(bulk_ref.at[k + ahead], rbulk_ref.at[k + ahead]))
        value = rbulk_ref[k].reshape((here + 1) * pair, HAD)
        rot_ref[k] = dot(value, signed).reshape(here + 1, pair, HAD)

    landed(r3_ref, last_maxima)
    peak = jnp.maximum(peak, jnp.max(r3_ref[...], axis=0))

    scales = jnp.sqrt(peak + 1e-06)
    inverse = 0.0625 / scales
    z_at = lax.broadcasted_iota(jnp.int32, (NZ, LANES), 0)
    l_at = lax.broadcasted_iota(jnp.int32, (NZ, LANES), 1)
    core_send = stage()
    core_recv = [stage() for _ in range(W)]
    for k in range(W):
        cols = slice(k * HAD, (k + 1) * HAD)
        pick = l_at == z_at * stride + k
        factor = jnp.concatenate(
            [
                jnp.sum(
                    jnp.where(pick, jnp.broadcast_to(inverse[g : g + 1], (NZ, LANES)), 0.0),
                    axis=1,
                    keepdims=True,
                )
                for g in range(CORES)
            ],
            axis=0,
        )
        factor = jnp.broadcast_to(factor, (pair, HAD))
        total = jnp.zeros((pair, HAD), F32)
        for j in range(here + 1):
            value = jnp.clip(rot_ref[k, j] * factor, -clip_level, clip_level)
            total = total + value.astype(BF16).astype(F32)
        acc_ref[0, :, cols] = total[0:NZ]
        acc_ref[1, :, cols] = total[NZ:pair]
        copy(
            acc_ref.at[1 - c, :, cols], racc_ref.at[:, cols], core_peer, core_send, core_recv[k]
        ).start()
    sent.append((racc_ref, core_send))

    w_at = lax.broadcasted_iota(jnp.int32, (W, LANES), 0)
    k_at = lax.broadcasted_iota(jnp.int32, (W, LANES), 1)
    own = jnp.broadcast_to(jnp.where(c == 0, scales[0:1], scales[1:2]), (W, LANES))
    own_scale = jnp.sum(
        jnp.where(k_at == z * stride + w_at, own, 0.0), axis=1, keepdims=True
    )

    for k in range(W):
        landed(racc_ref.at[:, k * HAD : (k + 1) * HAD], core_recv[k])
        for h in range(2):
            cols = slice(k * HAD + h * LANES, k * HAD + (h + 1) * LANES)
            zs_ref[:, h * W + k, :] = acc_ref[c, :, cols] + racc_ref[:, cols]

    index = stage()
    for j, o in enumerate(line):
        copy(
            zs_ref.at[lax.rem(z + o, NZ)], rz_ref.at[j], line_peer[o], index, index
        ).start()
    sent.append((rz_ref, index))
    own_part = zs_ref[z]
    landed(rz_ref, index)
    total = own_part + jnp.sum(rz_ref[...], axis=0)

    wide = jnp.concatenate([total[0:W], total[W : 2 * W]], axis=1)
    parts = split_three(wide * own_scale)
    table = table_ref[...]
    gradient = (dot(parts[0], table) + dot(parts[1], table)) + dot(parts[2], table)
    gradient = gradient * 0.0625 * sign_row
    grad_ref[y] = gradient
    updated, _, _ = adam(gradient, adam_ref[0], adam_ref[1], adam_ref[2])
    updated = updated.astype(BF16).astype(F32)
    near_ref[len(near), 0:W] = updated[:, 0:LANES]
    near_ref[len(near), W : 2 * W] = updated[:, LANES:HAD]

    far_sem = stage()
    near_sem = stage()
    mine = near_ref.at[len(near)]
    slots = {o % NZ: (near_ref.at[i], near_sem) for i, o in enumerate(near)}
    slots.update({o % NZ: (far_ref.at[i], far_sem) for i, o in enumerate(far)})
    for o in line:
        slot, index = slots[o]
        copy(mine, slot, line_peer[o], index, index).start()
    sent.append((far_ref, far_sem))
    if near:
        sent.append((near_ref.at[0 : len(near)], near_sem))
    column_sem = stage()
    for o in column:
        copy(
            grad_ref.at[y], grad_ref.at[y], device(0, o, 0, 0), column_sem, column_sem
        ).start()
    sent.append((grad_ref.at[0 : NY - 1], column_sem))

    WA = W // 2
    core_sems = (stage(), stage())
    sets = (ga_ref, gb_ref)
    extents = (NX, NY)

    def pack(wave, rows_ref):
        for k in range(W):
            both = jnp.concatenate([rows_ref[:, k, :], rows_ref[:, W + k, :]], axis=0)
            at = k if k < WA else k - WA
            sets[int(k >= WA)][c, wave, 0, :, at * LANES : (at + 1) * LANES] = both.astype(BF16)

    def along(wave, which, step):
        slots_ref = sets[which].at[c, wave]
        axis = which ^ step
        count = extents[which] if step else 1
        extent = extents[axis]
        send = stage()
        recv = {}
        for o in sorted(range(1, extent), key=lambda o: -ring_distance(o, extent)):
            recv[o] = stage()
            peer = device(o, 0, 0, 0) if axis == 0 else device(0, o, 0, 0)
            copy(
                slots_ref.at[0:count],
                slots_ref.at[count * o : count * (o + 1)],
                peer,
                send,
                recv[o],
            ).start()
        sent.append((slots_ref.at[count : count * extent], send))
        return recv

    def arrive(wave, which, step, recv):
        slots_ref = sets[which].at[c, wave]
        count = extents[which] if step else 1
        for o in sorted(recv, key=lambda o: ring_distance(o, len(recv) + 1)):
            piece = slots_ref.at[count * o : count * (o + 1)]
            landed(piece, recv[o])
            if step:
                copy(piece, piece, core_peer, core_sems[which], core_sems[which]).start()

    def pass_on(wave, which):
        piece = sets[which].at[c, wave, 0 : extents[which]]
        copy(piece, piece, core_peer, core_sems[which], core_sems[which]).start()

    if near:
        landed(near_ref.at[0 : len(near)], near_sem)
    pack(0, near_ref)
    near_one = [along(0, which, 0) for which in range(2)]
    landed(far_ref, far_sem)
    pack(1, far_ref)
    far_one = [along(1, which, 0) for which in range(2)]
    near_two = []
    far_two = []
    for which in range(2):
        arrive(0, which, 0, near_one[which])
        near_two.append(along(0, which, 1))
    for which in range(2):
        arrive(1, which, 0, far_one[which])
        far_two.append(along(1, which, 1))
    for wave in range(2):
        for which in range(2):
            pass_on(wave, which)
    for which in range(2):
        arrive(0, which, 1, near_two[which])
    for which in range(2):
        arrive(1, which, 1, far_two[which])
    landed(grad_ref.at[0 : NY - 1], column_sem)
    for which in range(2):
        landed(sets[which].at[1 - c], core_sems[which])
        sent.append((sets[which].at[c], core_sems[which]))

    for ref, index in sent:
        copy(ref, ref, core_peer, index, index).wait_send()


def write_kernel(
    sizes,
    ga_ref,
    gb_ref,
    grad_ref,
    master_ref,
    first_ref,
    second_ref,
    new_master_ref,
    new_first_ref,
    new_second_ref,
    out_ref,
    adam_ref,
):
    NX, NY, NZ, NB, W = sizes
    rows = NX * NZ * CORES
    near, far = line_offsets(NZ)
    dp = lax.axis_index("dp")
    y = lax.axis_index("outer")
    z = lax.rem(dp // CORES, NZ)
    x = dp // (CORES * NZ)

    for at in range(NY):
        begin = piece_start(sizes, at)
        for k in range(W):
            lo = (begin + k) * HAD
            adam_ref[0, k : k + 1, :] = master_ref[0:1, lo : lo + HAD]
            adam_ref[1, k : k + 1, :] = first_ref[0:1, lo : lo + HAD]
            adam_ref[2, k : k + 1, :] = second_ref[0:1, lo : lo + HAD]
        results = adam(grad_ref[at], adam_ref[0], adam_ref[1], adam_ref[2])
        end = piece_start(sizes, at + 1) if at < NY - 1 else NB
        for k in range(end - begin):
            lo = (begin + k) * HAD
            for ref, value in zip((new_master_ref, new_first_ref, new_second_ref), results):
                ref[0:1, lo : lo + HAD] = value[k : k + 1, :]

    slots = rows
    deep = NZ // 2
    r_at = lax.broadcasted_iota(jnp.int32, (rows, slots), 0)
    g_at = lax.broadcasted_iota(jnp.int32, (1, slots), 1)
    low = lax.rem(g_at, deep)
    ox = lax.rem(g_at // deep, NX)
    part = lax.rem(g_at // (deep * NX), 2)
    core = g_at // (deep * NX * 2)
    back = max(NZ // 4 - 1, 0)
    near_o = jnp.where(low == len(near), 0, low - back + (low >= back).astype(jnp.int32))
    oz = jnp.where(part == 0, near_o, low + NZ // 2 - back)
    source = (lax.rem(x - ox + NX, NX) * NZ + lax.rem(z - oz + NZ, NZ)) * CORES + core
    pick = (r_at == source).astype(F32).astype(BF16)
    for oy in range(NY):
        at = lax.rem(y + NY - oy, NY)
        begin = piece_start(sizes, at) * HAD
        tiles = []
        for h in range(2):
            parts = []
            for which, ref in enumerate((ga_ref, gb_ref)):
                value = jnp.concatenate(
                    [
                        ref[
                            core,
                            wave,
                            ox * NY + oy if which else oy * NX + ox,
                            h * deep : (h + 1) * deep,
                        ]
                        for core in range(CORES)
                        for wave in range(2)
                        for ox in range(NX)
                    ],
                    axis=0,
                )
                parts.append(dot(pick, value).astype(BF16))
            tiles.append(jnp.concatenate(parts, axis=1))
        for k in range(W):
            both = jnp.concatenate(
                [tile[:, k * LANES : (k + 1) * LANES] for tile in tiles], axis=1
            )
            cols = pl.ds(pl.multiple_of(begin + k * HAD, HAD), HAD)
            if k < W - 1:
                out_ref[:, cols] = both
            else:

                @pl.when((at == 0) | (at == NY - 1))
                def _():
                    out_ref[:, cols] = both


def build(mesh, NX, NZ, NB):
    NY = mesh.shape["outer"]
    W = -(-NB // NY)
    sizes = (NX, NY, NZ, NB, W)
    rows = NX * NZ * CORES
    pair = CORES * NZ
    n_plane = NX * NY - 1
    n_line = NZ - 1
    stages = 11 + 2 * W + 4 * (NX + NY)
    set_a = (W // 2) * LANES
    near, far = line_offsets(NZ)
    width = NB * HAD
    piece = W * HAD
    scratch = [
        pltpu.VMEM((rows, width), BF16),
        pltpu.VMEM((1, HAD), jnp.int32),
        pltpu.VMEM((3, 1, piece), F32),
        pltpu.VMEM((HAD, HAD), BF16),
        pltpu.VMEM((HAD, HAD), BF16),
        pltpu.VMEM((3, W, HAD), F32),
        pltpu.VMEM((W, NY, NX, pair, HAD), BF16),
        pltpu.VMEM((W, n_plane + 1, pair, HAD), BF16),
        pltpu.VMEM((W, n_plane + 1, pair, HAD), F32),
        pltpu.VMEM((NY, NX, CORES, LANES), F32),
        pltpu.VMEM((n_plane, CORES, LANES), F32),
        pltpu.VMEM((CORES, LANES), F32),
        pltpu.VMEM((CORES, LANES), F32),
        pltpu.VMEM((CORES, LANES), F32),
        pltpu.VMEM((n_line, CORES, LANES), F32),
        pltpu.VMEM((CORES, NZ, piece), F32),
        pltpu.VMEM((NZ, piece), F32),
        pltpu.VMEM((NZ, 2 * W, LANES), F32),
        pltpu.VMEM((n_line, 2 * W, LANES), F32),
        pltpu.VMEM((len(near) + 1, 2 * W, LANES), F32),
        pltpu.VMEM((len(far), 2 * W, LANES), F32),
        pltpu.SemaphoreType.DMA((5,)),
        pltpu.SemaphoreType.DMA((stages,)),
        pltpu.SemaphoreType.DMA((stages,)),
    ]
    vmem = pl.BlockSpec(memory_space=pltpu.VMEM)
    row = jax.ShapeDtypeStruct((1, width), F32)

    def per_device(replica_grads, hadamard_signs, master_rows, first_moment, second_moment):
        first_set, second_set, gradients = pl.pallas_call(
            functools.partial(exchange_kernel, sizes),
            out_shape=(
                pltpu.VMEM((CORES, 2, n_plane + 1, NZ, set_a), BF16),
                pltpu.VMEM((CORES, 2, n_plane + 1, NZ, piece // 2 - set_a), BF16),
                pltpu.VMEM((NY, W, HAD), F32),
            ),
            in_specs=[pl.BlockSpec(memory_space=pltpu.HBM)] * 5,
            out_specs=(vmem, vmem, vmem),
            scratch_shapes=scratch,
            compiler_params=pltpu.CompilerParams(
                collective_id=0, has_side_effects=True, vmem_limit_bytes=40 * 2**20
            ),
        )(
            *[
                pltpu.with_memory_space_constraint(array, pltpu.HBM)
                for array in (
                    replica_grads,
                    hadamard_signs.reshape(1, HAD),
                    master_rows,
                    first_moment,
                    second_moment,
                )
            ]
        )
        return pl.pallas_call(
            functools.partial(write_kernel, sizes),
            out_shape=(row, row, row, jax.ShapeDtypeStruct((rows, width), BF16)),
            in_specs=[vmem] * 6,
            out_specs=(vmem,) * 4,
            scratch_shapes=[pltpu.VMEM((3, W, HAD), F32)],
            compiler_params=pltpu.CompilerParams(vmem_limit_bytes=20 * 2**20),
        )(first_set, second_set, gradients, master_rows, first_moment, second_moment)

    in_specs = (P("dp", "outer", None, None), P(), P("dp", None), P("dp", None), P("dp", None))
    out_specs = (P("dp", None), P("dp", None), P("dp", None), P())
    return jax.shard_map(
        per_device, mesh=mesh, in_specs=in_specs, out_specs=out_specs, check_vma=False
    )


def solution(mesh):
    return build(mesh, 4, 16, 18)
```

```python
import functools

import jax
import jax.numpy as jnp
from jax import lax
from jax.experimental import pallas as pl
from jax.experimental.pallas import tpu as pltpu
from jax.sharding import PartitionSpec as P

HAD = 256
LANES = 128
STEP = 1000
CORES = 2

beta_one = 0.9
beta_two = 0.95
rate = 0.001
decay = 0.1
tiny_eps = 1e-08
clip_level = 1.5
first_fix = 1.0 - beta_one**STEP
second_fix = 1.0 - beta_two**STEP

F32 = jnp.float32
BF16 = jnp.bfloat16
MESH = pl.DeviceIdType.MESH


def ring_distance(offset, size):
    return min(offset, size - offset)


def hadamard(dtype):
    bits = lax.broadcasted_iota(jnp.int32, (HAD, HAD), 0) & lax.broadcasted_iota(
        jnp.int32, (HAD, HAD), 1
    )
    bits = bits ^ (bits >> 4)
    bits = bits ^ (bits >> 2)
    bits = bits ^ (bits >> 1)
    return (1 - 2 * (bits & 1)).astype(F32).astype(dtype)


def split_three(value):
    high = value.astype(BF16)
    rest = value - high.astype(F32)
    middle = rest.astype(BF16)
    low = (rest - middle.astype(F32)).astype(BF16)
    return high, middle, low


def dot(a, b):
    return jnp.dot(a, b, preferred_element_type=F32)


def adam(gradient, master, first, second):
    new_first = beta_one * first + (1.0 - beta_one) * gradient
    new_second = beta_two * second + (1.0 - beta_two) * gradient * gradient
    update = (
        new_first * (1.0 / first_fix) / (jnp.sqrt(new_second * (1.0 / second_fix)) + tiny_eps)
        + decay * master
    )
    return master - rate * update, new_first, new_second


def piece_start(sizes, at):
    NX, NY, NZ, NB, W = sizes
    return (at * (NB - W) + NY - 2) // (NY - 1)


def plane_offsets(NX, NY):
    plane = [(ox, oy) for oy in range(NY) for ox in range(NX) if ox or oy]
    return sorted(plane, key=lambda o: -plane_hops(NX, NY, o))


def plane_hops(NX, NY, o):
    return ring_distance(o[0], NX) + ring_distance(o[1], NY)


def line_offsets(NZ):
    back = max(NZ // 4 - 1, 0)
    near = [o for o in range(-back, NZ // 2 - back) if o]
    far = list(range(NZ // 2 - back, NZ - back))
    return near, far


def exchange_kernel(
    sizes,
    grads_hbm,
    signs_hbm,
    master_hbm,
    first_hbm,
    second_hbm,
    ga_ref,
    gb_ref,
    grad_ref,
    x_ref,
    signs_ref,
    state_ref,
    table_ref,
    signed_ref,
    adam_ref,
    bulk_ref,
    rbulk_ref,
    rot_ref,
    m1_ref,
    r1_ref,
    m2_ref,
    r2_ref,
    m3_ref,
    r3_ref,
    acc_ref,
    racc_ref,
    zs_ref,
    rz_ref,
    near_ref,
    far_ref,
    load_sems,
    send_sems,
    recv_sems,
):
    NX, NY, NZ, NB, W = sizes
    rows = NX * NZ * CORES
    pair = CORES * NZ
    stride = LANES // NZ

    dp = lax.axis_index("dp")
    y = lax.axis_index("outer")
    c = lax.rem(dp, CORES)
    z = lax.rem(dp // CORES, NZ)
    x = dp // (CORES * NZ)

    def first_block(at):
        return piece_start(sizes, at)

    def device(dx, dy, dz, dc):
        px = lax.rem(x + dx, NX)
        py = lax.rem(y + dy, NY)
        pz = lax.rem(z + dz, NZ)
        pc = lax.rem(c + dc, CORES)
        return ((px * NZ + pz) * CORES + pc, py)

    plane = plane_offsets(NX, NY)
    near, far = line_offsets(NZ)
    line = sorted([o % NZ for o in near + far], key=lambda o: -ring_distance(o, NZ))
    column = list(range(1, NY))
    core_peer = device(0, 0, 0, 1)
    plane_peer = [device(o[0], o[1], 0, 0) for o in plane]
    line_peer = {o: device(0, 0, o, 0) for o in line}
    here = len(plane)

    grads_load = pltpu.make_async_copy(grads_hbm.at[0, 0], x_ref, load_sems.at[0])
    grads_load.start()
    barrier = pltpu.get_barrier_semaphore()
    peers = [line_peer[o] for o in line] + plane_peer + [core_peer]
    for peer in peers:
        pl.semaphore_signal(barrier, inc=1, device_id=peer, device_id_type=MESH)

    begin = pl.multiple_of(first_block(y) * HAD, HAD)
    loads = [pltpu.make_async_copy(signs_hbm, signs_ref, load_sems.at[1])]
    for i, hbm in enumerate((master_hbm, first_hbm, second_hbm)):
        loads.append(
            pltpu.make_async_copy(
                hbm.at[:, pl.ds(begin, W * HAD)], state_ref.at[i], load_sems.at[2 + i]
            )
        )
    for load in loads:
        load.start()

    counter = {True: 0, False: 0}
    sent = []

    def copy(src, dst, peer, send, recv):
        return pltpu.make_async_remote_copy(
            src_ref=src,
            dst_ref=dst,
            send_sem=send_sems.at[send],
            recv_sem=recv_sems.at[recv],
            device_id=peer,
            device_id_type=MESH,
        )

    def stage(send):
        counter[send] += 1
        return counter[send] - 1

    def landed(ref, index):
        copy(ref, ref, core_peer, 0, index).wait_recv()

    p_at = lax.broadcasted_iota(jnp.int32, (rows, rows), 0)
    r_at = lax.broadcasted_iota(jnp.int32, (1, rows), 1)
    r_core = lax.rem(r_at, CORES)
    r_z = lax.rem(r_at // CORES, NZ)
    r_x = r_at // pair
    order = (p_at == r_x * pair + r_core * NZ + r_z).astype(F32).astype(BF16)

    table = hadamard(BF16)
    table_ref[...] = table

    grads_load.wait()

    lane = lax.rem(lax.broadcasted_iota(jnp.int32, (1, LANES), 1), stride)
    picks = [
        jnp.broadcast_to((lane == k).astype(F32), (HAD, LANES)).astype(BF16) for k in range(W)
    ]
    sums = [jnp.zeros((rows, LANES), F32) for _ in range(NY)]
    for block in range(NB):
        value = dot(order, x_ref[:, block * HAD : (block + 1) * HAD])
        square = value * value
        high = square.astype(BF16)
        low = (square - high.astype(F32)).astype(BF16)
        both = jnp.concatenate([high, low], axis=0)
        value = value.astype(BF16).reshape(NX, pair, HAD)
        for at in range(NY):
            k = block - first_block(at)
            if 0 <= k < W:
                part = dot(both, picks[k])
                sums[at] = sums[at] + (part[0:rows] + part[rows : 2 * rows])
                bulk_ref[k, at] = value
    row_at = lax.broadcasted_iota(jnp.int32, (rows, LANES), 0)
    lane_at = lax.broadcasted_iota(jnp.int32, (rows, LANES), 1)
    mine = row_at % NZ == lane_at // stride
    for at in range(NY):
        packed = jnp.where(mine, sums[at], 0.0).reshape(NX * CORES, NZ, LANES)
        packed = jnp.sum(packed, axis=1) * (1.0 / HAD)
        for px in range(NX):
            m1_ref[at, px] = packed[px * CORES : (px + 1) * CORES]

    pl.semaphore_wait(barrier, len(peers))

    def over_plane(parts_ref, slots_ref, send):
        recv = stage(False)
        for j, o in enumerate(plane):
            piece = parts_ref.at[lax.rem(y + o[1], NY), lax.rem(x + o[0], NX)]
            copy(piece, slots_ref.at[j], plane_peer[j], send, recv).start()
        return recv

    maxima_send = stage(True)
    first_maxima = over_plane(m1_ref, r1_ref, maxima_send)
    sent.append((r1_ref, maxima_send))
    bulk_send = stage(True)
    ahead = 3
    waves = [over_plane(bulk_ref.at[k], rbulk_ref.at[k], bulk_send) for k in range(ahead - 1)]
    for k in range(W):
        rbulk_ref[k, here] = bulk_ref[k, y, x]

    diagonal = lax.broadcasted_iota(jnp.int32, (HAD, HAD), 0) == lax.broadcasted_iota(
        jnp.int32, (HAD, HAD), 1
    )
    for load in loads:
        load.wait()
    sign_row = signs_ref[...].astype(F32)
    signed_ref[...] = dot(
        jnp.where(diagonal, sign_row, 0.0).astype(BF16), table
    ).astype(BF16)
    for k in range(W):
        for i in range(3):
            adam_ref[i, k : k + 1, :] = state_ref[i, :, k * HAD : (k + 1) * HAD]

    landed(r1_ref, first_maxima)
    waves.append(over_plane(bulk_ref.at[ahead - 1], rbulk_ref.at[ahead - 1], bulk_send))
    peak = jnp.maximum(m1_ref[y, x], jnp.max(r1_ref[...], axis=0))
    m2_ref[...] = peak
    send, recv = stage(True), stage(False)
    copy(m2_ref, r2_ref, core_peer, send, recv).start()
    sent.append((r2_ref, send))
    landed(r2_ref, recv)
    peak = jnp.maximum(peak, r2_ref[...])
    m3_ref[...] = peak
    send, last_maxima = stage(True), stage(False)
    for j, o in enumerate(line):
        copy(m3_ref, r3_ref.at[j], line_peer[o], send, last_maxima).start()
    sent.append((r3_ref, send))

    signed = signed_ref[...]
    for k in range(W):
        landed(rbulk_ref.at[k, 0:here], waves[k])
        if k + ahead < W:
            waves.append(over_plane(bulk_ref.at[k + ahead], rbulk_ref.at[k + ahead], bulk_send))
        value = rbulk_ref[k].reshape((here + 1) * pair, HAD)
        rot_ref[k] = dot(value, signed).reshape(here + 1, pair, HAD)

    sent.append((rbulk_ref.at[:, 0:here], bulk_send))
    landed(r3_ref, last_maxima)
    peak = jnp.maximum(peak, jnp.max(r3_ref[...], axis=0))

    scales = jnp.sqrt(peak + 1e-06)
    inverse = 0.0625 / scales
    z_at = lax.broadcasted_iota(jnp.int32, (NZ, LANES), 0)
    l_at = lax.broadcasted_iota(jnp.int32, (NZ, LANES), 1)
    core_send = stage(True)
    core_recv = [stage(False) for _ in range(W)]
    for k in range(W):
        cols = slice(k * HAD, (k + 1) * HAD)
        pick = l_at == z_at * stride + k
        factor = jnp.concatenate(
            [
                jnp.sum(
                    jnp.where(pick, jnp.broadcast_to(inverse[g : g + 1], (NZ, LANES)), 0.0),
                    axis=1,
                    keepdims=True,
                )
                for g in range(CORES)
            ],
            axis=0,
        )
        factor = jnp.broadcast_to(factor, (pair, HAD))
        total = jnp.zeros((pair, HAD), F32)
        for j in range(here + 1):
            value = jnp.clip(rot_ref[k, j] * factor, -clip_level, clip_level)
            total = total + value.astype(BF16).astype(F32)
        acc_ref[0, :, cols] = total[0:NZ]
        acc_ref[1, :, cols] = total[NZ:pair]
        copy(
            acc_ref.at[1 - c, :, cols], racc_ref.at[:, cols], core_peer, core_send, core_recv[k]
        ).start()
    sent.append((racc_ref, core_send))

    w_at = lax.broadcasted_iota(jnp.int32, (W, LANES), 0)
    k_at = lax.broadcasted_iota(jnp.int32, (W, LANES), 1)
    own = jnp.broadcast_to(jnp.where(c == 0, scales[0:1], scales[1:2]), (W, LANES))
    own_scale = jnp.sum(
        jnp.where(k_at == z * stride + w_at, own, 0.0), axis=1, keepdims=True
    )

    for k in range(W):
        landed(racc_ref.at[:, k * HAD : (k + 1) * HAD], core_recv[k])
        for h in range(2):
            cols = slice(k * HAD + h * LANES, k * HAD + (h + 1) * LANES)
            zs_ref[:, h * W + k, :] = acc_ref[c, :, cols] + racc_ref[:, cols]

    send, recv = stage(True), stage(False)
    for j, o in enumerate(line):
        copy(zs_ref.at[lax.rem(z + o, NZ)], rz_ref.at[j], line_peer[o], send, recv).start()
    sent.append((rz_ref, send))
    own_part = zs_ref[z]
    landed(rz_ref, recv)
    total = own_part + jnp.sum(rz_ref[...], axis=0)

    wide = jnp.concatenate([total[0:W], total[W : 2 * W]], axis=1)
    parts = split_three(wide * own_scale)
    table = table_ref[...]
    gradient = (dot(parts[0], table) + dot(parts[1], table)) + dot(parts[2], table)
    gradient = gradient * 0.0625 * sign_row
    grad_ref[y] = gradient
    updated, _, _ = adam(gradient, adam_ref[0], adam_ref[1], adam_ref[2])
    updated = updated.astype(BF16).astype(F32)
    near_ref[len(near), 0:W] = updated[:, 0:LANES]
    near_ref[len(near), W : 2 * W] = updated[:, LANES:HAD]

    far_send, far_recv = stage(True), stage(False)
    near_send, near_recv = stage(True), stage(False)
    mine = near_ref.at[len(near)]
    slots = {o % NZ: (near_ref.at[i], near_send, near_recv) for i, o in enumerate(near)}
    slots.update({o % NZ: (far_ref.at[i], far_send, far_recv) for i, o in enumerate(far)})
    for o in line:
        slot, send, recv = slots[o]
        copy(mine, slot, line_peer[o], send, recv).start()
    sent.append((far_ref, far_send))
    if near:
        sent.append((near_ref.at[0 : len(near)], near_send))
    column_send, column_recv = stage(True), stage(False)
    for o in column:
        copy(
            grad_ref.at[y], grad_ref.at[y], device(0, o, 0, 0), column_send, column_recv
        ).start()
    sent.append((grad_ref.at[0 : NY - 1], column_send))

    WA = W // 2
    core_sends = (stage(True), stage(True))
    core_recvs = (stage(False), stage(False))
    step_sends = [[stage(True) for _ in range(2)] for _ in range(2)]
    sets = (ga_ref, gb_ref)
    extents = (NX, NY)

    def pack(wave, rows_ref):
        for k in range(W):
            both = jnp.concatenate([rows_ref[:, k, :], rows_ref[:, W + k, :]], axis=0)
            at = k if k < WA else k - WA
            sets[int(k >= WA)][c, wave, 0, :, at * LANES : (at + 1) * LANES] = both.astype(BF16)

    def along(wave, which, step):
        slots_ref = sets[which].at[c, wave]
        axis = which ^ step
        count = extents[which] if step else 1
        extent = extents[axis]
        send = step_sends[which][step]
        first = stage(False)
        recv = {}
        for o in sorted(range(1, extent), key=lambda o: -ring_distance(o, extent)):
            recv[o] = stage(False) if step and recv else first
            peer = device(o, 0, 0, 0) if axis == 0 else device(0, o, 0, 0)
            copy(
                slots_ref.at[0:count],
                slots_ref.at[count * o : count * (o + 1)],
                peer,
                send,
                recv[o],
            ).start()
        if wave:
            sent.append((sets[which].at[c, :, count : count * extent], send))
        return recv

    def pass_on(which, piece):
        copy(piece, piece, core_peer, core_sends[which], core_recvs[which]).start()

    def arrive(wave, which, step, recv):
        slots_ref = sets[which].at[c, wave]
        if step == 0:
            landed(slots_ref.at[1 : len(recv) + 1], recv[1])
            return
        count = extents[which]
        for o in sorted(recv, key=lambda o: ring_distance(o, len(recv) + 1)):
            piece = slots_ref.at[count * o : count * (o + 1)]
            landed(piece, recv[o])
            pass_on(which, piece)

    if near:
        landed(near_ref.at[0 : len(near)], near_recv)
    pack(0, near_ref)
    near_one = [along(0, which, 0) for which in range(2)]
    landed(far_ref, far_recv)
    pack(1, far_ref)
    far_one = [along(1, which, 0) for which in range(2)]
    near_two = []
    far_two = []
    for which in range(2):
        arrive(0, which, 0, near_one[which])
        near_two.append(along(0, which, 1))
    for which in range(2):
        arrive(1, which, 0, far_one[which])
        far_two.append(along(1, which, 1))
    for wave in range(2):
        for which in range(2):
            pass_on(which, sets[which].at[c, wave, 0 : extents[which]])
    for which in range(2):
        arrive(0, which, 1, near_two[which])
    for which in range(2):
        arrive(1, which, 1, far_two[which])
    landed(grad_ref.at[0 : NY - 1], column_recv)
    for which in range(2):
        landed(sets[which].at[1 - c], core_recvs[which])
        sent.append((sets[which].at[c], core_sends[which]))

    for ref, index in sent:
        copy(ref, ref, core_peer, index, 0).wait_send()


def write_kernel(
    sizes,
    ga_ref,
    gb_ref,
    grad_ref,
    master_ref,
    first_ref,
    second_ref,
    new_master_ref,
    new_first_ref,
    new_second_ref,
    out_hbm,
    adam_ref,
    out_ref,
    out_sems,
):
    NX, NY, NZ, NB, W = sizes
    rows = NX * NZ * CORES
    near, far = line_offsets(NZ)
    dp = lax.axis_index("dp")
    y = lax.axis_index("outer")
    z = lax.rem(dp // CORES, NZ)
    x = dp // (CORES * NZ)

    slots = rows
    deep = NZ // 2
    r_at = lax.broadcasted_iota(jnp.int32, (rows, slots), 0)
    g_at = lax.broadcasted_iota(jnp.int32, (1, slots), 1)
    low = lax.rem(g_at, deep)
    ox = lax.rem(g_at // deep, NX)
    part = lax.rem(g_at // (deep * NX), 2)
    core = g_at // (deep * NX * 2)
    back = max(NZ // 4 - 1, 0)
    near_o = jnp.where(low == len(near), 0, low - back + (low >= back).astype(jnp.int32))
    oz = jnp.where(part == 0, near_o, low + NZ // 2 - back)
    source = (lax.rem(x - ox + NX, NX) * NZ + lax.rem(z - oz + NZ, NZ)) * CORES + core
    pick = (r_at == source).astype(F32).astype(BF16)
    most = []
    lasts = []
    for oy in range(NY):
        at = lax.rem(y + NY - oy, NY)
        begin = piece_start(sizes, at) * HAD
        tiles = []
        for h in range(2):
            parts = []
            for which, ref in enumerate((ga_ref, gb_ref)):
                value = jnp.concatenate(
                    [
                        ref[
                            core,
                            wave,
                            ox * NY + oy if which else oy * NX + ox,
                            h * deep : (h + 1) * deep,
                        ]
                        for core in range(CORES)
                        for wave in range(2)
                        for ox in range(NX)
                    ],
                    axis=0,
                )
                parts.append(dot(pick, value).astype(BF16))
            tiles.append(jnp.concatenate(parts, axis=1))
        for k in range(W):
            both = jnp.concatenate(
                [tile[:, k * LANES : (k + 1) * LANES] for tile in tiles], axis=1
            )
            out_ref[oy, :, k * HAD : (k + 1) * HAD] = both
        kept = (W - 1) * HAD
        cols = pl.ds(pl.multiple_of(begin, HAD), kept)
        most.append(
            pltpu.make_async_copy(out_ref.at[oy, :, 0:kept], out_hbm.at[:, cols], out_sems.at[0, oy])
        )
        most[oy].start()
        cols = pl.ds(pl.multiple_of(begin + kept, HAD), HAD)
        last = pltpu.make_async_copy(
            out_ref.at[oy, :, kept : W * HAD], out_hbm.at[:, cols], out_sems.at[1, oy]
        )
        lasts.append(((at == 0) | (at == NY - 1), last))

        @pl.when(lasts[oy][0])
        def _():
            lasts[oy][1].start()

    for at in range(NY):
        begin = piece_start(sizes, at)
        for k in range(W):
            lo = (begin + k) * HAD
            adam_ref[0, k : k + 1, :] = master_ref[0:1, lo : lo + HAD]
            adam_ref[1, k : k + 1, :] = first_ref[0:1, lo : lo + HAD]
            adam_ref[2, k : k + 1, :] = second_ref[0:1, lo : lo + HAD]
        results = adam(grad_ref[at], adam_ref[0], adam_ref[1], adam_ref[2])
        end = piece_start(sizes, at + 1) if at < NY - 1 else NB
        for k in range(end - begin):
            lo = (begin + k) * HAD
            for ref, value in zip((new_master_ref, new_first_ref, new_second_ref), results):
                ref[0:1, lo : lo + HAD] = value[k : k + 1, :]

    for oy in range(NY):
        most[oy].wait()

        @pl.when(lasts[oy][0])
        def _():
            lasts[oy][1].wait()


def build(mesh, NX, NZ, NB):
    NY = mesh.shape["outer"]
    W = -(-NB // NY)
    sizes = (NX, NY, NZ, NB, W)
    rows = NX * NZ * CORES
    pair = CORES * NZ
    n_plane = NX * NY - 1
    n_line = NZ - 1
    sends = 15
    recvs = 10 + 2 * W + 4 + 2 * (NX + NY - 2)
    set_a = (W // 2) * LANES
    near, far = line_offsets(NZ)
    width = NB * HAD
    piece = W * HAD
    scratch = [
        pltpu.VMEM((rows, width), BF16),
        pltpu.VMEM((1, HAD), jnp.int32),
        pltpu.VMEM((3, 1, piece), F32),
        pltpu.VMEM((HAD, HAD), BF16),
        pltpu.VMEM((HAD, HAD), BF16),
        pltpu.VMEM((3, W, HAD), F32),
        pltpu.VMEM((W, NY, NX, pair, HAD), BF16),
        pltpu.VMEM((W, n_plane + 1, pair, HAD), BF16),
        pltpu.VMEM((W, n_plane + 1, pair, HAD), F32),
        pltpu.VMEM((NY, NX, CORES, LANES), F32),
        pltpu.VMEM((n_plane, CORES, LANES), F32),
        pltpu.VMEM((CORES, LANES), F32),
        pltpu.VMEM((CORES, LANES), F32),
        pltpu.VMEM((CORES, LANES), F32),
        pltpu.VMEM((n_line, CORES, LANES), F32),
        pltpu.VMEM((CORES, NZ, piece), F32),
        pltpu.VMEM((NZ, piece), F32),
        pltpu.VMEM((NZ, 2 * W, LANES), F32),
        pltpu.VMEM((n_line, 2 * W, LANES), F32),
        pltpu.VMEM((len(near) + 1, 2 * W, LANES), F32),
        pltpu.VMEM((len(far), 2 * W, LANES), F32),
        pltpu.SemaphoreType.DMA((5,)),
        pltpu.SemaphoreType.DMA((sends,)),
        pltpu.SemaphoreType.DMA((recvs,)),
    ]
    vmem = pl.BlockSpec(memory_space=pltpu.VMEM)
    row = jax.ShapeDtypeStruct((1, width), F32)

    def per_device(replica_grads, hadamard_signs, master_rows, first_moment, second_moment):
        first_set, second_set, gradients = pl.pallas_call(
            functools.partial(exchange_kernel, sizes),
            out_shape=(
                pltpu.VMEM((CORES, 2, n_plane + 1, NZ, set_a), BF16),
                pltpu.VMEM((CORES, 2, n_plane + 1, NZ, piece // 2 - set_a), BF16),
                pltpu.VMEM((NY, W, HAD), F32),
            ),
            in_specs=[pl.BlockSpec(memory_space=pltpu.HBM)] * 5,
            out_specs=(vmem, vmem, vmem),
            scratch_shapes=scratch,
            compiler_params=pltpu.CompilerParams(
                collective_id=0, has_side_effects=True, vmem_limit_bytes=40 * 2**20
            ),
        )(
            *[
                pltpu.with_memory_space_constraint(array, pltpu.HBM)
                for array in (
                    replica_grads,
                    hadamard_signs.reshape(1, HAD),
                    master_rows,
                    first_moment,
                    second_moment,
                )
            ]
        )
        return pl.pallas_call(
            functools.partial(write_kernel, sizes),
            out_shape=(row, row, row, jax.ShapeDtypeStruct((rows, width), BF16)),
            in_specs=[vmem] * 6,
            out_specs=(vmem,) * 3 + (pl.BlockSpec(memory_space=pl.ANY),),
            scratch_shapes=[
                pltpu.VMEM((3, W, HAD), F32),
                pltpu.VMEM((NY, rows, piece), BF16),
                pltpu.SemaphoreType.DMA((2, NY)),
            ],
            compiler_params=pltpu.CompilerParams(vmem_limit_bytes=20 * 2**20),
        )(first_set, second_set, gradients, master_rows, first_moment, second_moment)

    in_specs = (P("dp", "outer", None, None), P(), P("dp", None), P("dp", None), P("dp", None))
    out_specs = (P("dp", None), P("dp", None), P("dp", None), P())
    return jax.shard_map(
        per_device, mesh=mesh, in_specs=in_specs, out_specs=out_specs, check_vma=False
    )


def solution(mesh):
    return build(mesh, 4, 16, 18)
```

```python
import functools

import jax
import jax.numpy as jnp
from jax import lax
from jax.experimental import pallas as pl
from jax.experimental.pallas import tpu as pltpu
from jax.sharding import PartitionSpec as P

HAD = 256
LANES = 128
STEP = 1000
CORES = 2

beta_one = 0.9
beta_two = 0.95
rate = 0.001
decay = 0.1
tiny_eps = 1e-08
clip_level = 1.5
first_fix = 1.0 - beta_one**STEP
second_fix = 1.0 - beta_two**STEP

F32 = jnp.float32
BF16 = jnp.bfloat16
MESH = pl.DeviceIdType.MESH


def ring_distance(offset, size):
    return min(offset, size - offset)


def hadamard(dtype):
    bits = lax.broadcasted_iota(jnp.int32, (HAD, HAD), 0) & lax.broadcasted_iota(
        jnp.int32, (HAD, HAD), 1
    )
    bits = bits ^ (bits >> 4)
    bits = bits ^ (bits >> 2)
    bits = bits ^ (bits >> 1)
    return (1 - 2 * (bits & 1)).astype(F32).astype(dtype)


def split_three(value):
    high = value.astype(BF16)
    rest = value - high.astype(F32)
    middle = rest.astype(BF16)
    low = (rest - middle.astype(F32)).astype(BF16)
    return high, middle, low


def dot(a, b):
    return jnp.dot(a, b, preferred_element_type=F32)


def adam(gradient, master, first, second):
    new_first = beta_one * first + (1.0 - beta_one) * gradient
    new_second = beta_two * second + (1.0 - beta_two) * gradient * gradient
    update = (
        new_first * (1.0 / first_fix) / (jnp.sqrt(new_second * (1.0 / second_fix)) + tiny_eps)
        + decay * master
    )
    return master - rate * update, new_first, new_second


def piece_start(sizes, at):
    NX, NY, NZ, NB, W = sizes
    return (at * (NB - W) + NY - 2) // (NY - 1)


def plane_offsets(NX, NY):
    plane = [(ox, oy) for oy in range(NY) for ox in range(NX) if ox or oy]
    return sorted(plane, key=lambda o: -plane_hops(NX, NY, o))


def plane_hops(NX, NY, o):
    return ring_distance(o[0], NX) + ring_distance(o[1], NY)


def line_offsets(NZ):
    back = max(NZ // 4 - 1, 0)
    near = [o for o in range(-back, NZ // 2 - back) if o]
    far = list(range(NZ // 2 - back, NZ - back))
    return near, far


def exchange_kernel(
    sizes,
    grads_hbm,
    signs_hbm,
    master_hbm,
    first_hbm,
    second_hbm,
    ga_ref,
    gb_ref,
    grad_ref,
    x_ref,
    signs_ref,
    state_ref,
    table_ref,
    signed_ref,
    adam_ref,
    bulk_ref,
    rbulk_ref,
    rot_ref,
    m1_ref,
    r1_ref,
    m2_ref,
    r2_ref,
    m3_ref,
    r3_ref,
    acc_ref,
    racc_ref,
    zs_ref,
    rz_ref,
    near_ref,
    far_ref,
    load_sems,
    send_sems,
    recv_sems,
):
    NX, NY, NZ, NB, W = sizes
    rows = NX * NZ * CORES
    pair = CORES * NZ
    stride = LANES // NZ

    dp = lax.axis_index("dp")
    y = lax.axis_index("outer")
    c = lax.rem(dp, CORES)
    z = lax.rem(dp // CORES, NZ)
    x = dp // (CORES * NZ)

    def first_block(at):
        return piece_start(sizes, at)

    def device(dx, dy, dz, dc):
        px = lax.rem(x + dx, NX)
        py = lax.rem(y + dy, NY)
        pz = lax.rem(z + dz, NZ)
        pc = lax.rem(c + dc, CORES)
        return ((px * NZ + pz) * CORES + pc, py)

    plane = plane_offsets(NX, NY)
    near, far = line_offsets(NZ)
    line = sorted([o % NZ for o in near + far], key=lambda o: -ring_distance(o, NZ))
    column = list(range(1, NY))
    core_peer = device(0, 0, 0, 1)
    plane_peer = [device(o[0], o[1], 0, 0) for o in plane]
    line_peer = {o: device(0, 0, o, 0) for o in line}
    here = len(plane)

    grads_load = pltpu.make_async_copy(grads_hbm.at[0, 0], x_ref, load_sems.at[0])
    grads_load.start()
    barrier = pltpu.get_barrier_semaphore()
    peers = [line_peer[o] for o in line] + plane_peer + [core_peer]
    for peer in peers:
        pl.semaphore_signal(barrier, inc=1, device_id=peer, device_id_type=MESH)

    begin = pl.multiple_of(first_block(y) * HAD, HAD)
    loads = [pltpu.make_async_copy(signs_hbm, signs_ref, load_sems.at[1])]
    for i, hbm in enumerate((master_hbm, first_hbm, second_hbm)):
        loads.append(
            pltpu.make_async_copy(
                hbm.at[:, pl.ds(begin, W * HAD)], state_ref.at[i], load_sems.at[2 + i]
            )
        )
    for load in loads:
        load.start()

    counter = {True: 0, False: 0}
    sent = []

    def copy(src, dst, peer, send, recv):
        return pltpu.make_async_remote_copy(
            src_ref=src,
            dst_ref=dst,
            send_sem=send_sems.at[send],
            recv_sem=recv_sems.at[recv],
            device_id=peer,
            device_id_type=MESH,
        )

    def stage(send):
        counter[send] += 1
        return counter[send] - 1

    def landed(ref, index):
        copy(ref, ref, core_peer, 0, index).wait_recv()

    p_at = lax.broadcasted_iota(jnp.int32, (rows, rows), 0)
    r_at = lax.broadcasted_iota(jnp.int32, (1, rows), 1)
    r_core = lax.rem(r_at, CORES)
    r_z = lax.rem(r_at // CORES, NZ)
    r_x = r_at // pair
    order = (p_at == r_x * pair + r_core * NZ + r_z).astype(F32).astype(BF16)

    table = hadamard(BF16)
    table_ref[...] = table

    grads_load.wait()

    lane = lax.rem(lax.broadcasted_iota(jnp.int32, (1, LANES), 1), stride)
    picks = [
        jnp.broadcast_to((lane == k).astype(F32), (HAD, LANES)).astype(BF16) for k in range(W)
    ]
    sums = [jnp.zeros((rows, LANES), F32) for _ in range(NY)]
    for block in range(NB):
        value = dot(order, x_ref[:, block * HAD : (block + 1) * HAD])
        square = value * value
        high = square.astype(BF16)
        low = (square - high.astype(F32)).astype(BF16)
        both = jnp.concatenate([high, low], axis=0)
        value = value.astype(BF16).reshape(NX, pair, HAD)
        for at in range(NY):
            k = block - first_block(at)
            if 0 <= k < W:
                part = dot(both, picks[k])
                sums[at] = sums[at] + (part[0:rows] + part[rows : 2 * rows])
                bulk_ref[k, at] = value
    row_at = lax.broadcasted_iota(jnp.int32, (rows, LANES), 0)
    lane_at = lax.broadcasted_iota(jnp.int32, (rows, LANES), 1)
    mine = row_at % NZ == lane_at // stride
    for at in range(NY):
        packed = jnp.where(mine, sums[at], 0.0).reshape(NX * CORES, NZ, LANES)
        packed = jnp.sum(packed, axis=1) * (1.0 / HAD)
        for px in range(NX):
            m1_ref[at, px] = packed[px * CORES : (px + 1) * CORES]

    pl.semaphore_wait(barrier, len(peers))

    def outer_piece(at):
        return (at == 0) | (at == NY - 1)

    def over_plane(parts_ref, slots_ref, send, outer_only=False):
        recv = stage(False)
        for j, o in enumerate(plane):
            at = lax.rem(y + o[1], NY)
            piece = parts_ref.at[at, lax.rem(x + o[0], NX)]
            message = copy(piece, slots_ref.at[j], plane_peer[j], send, recv)
            if outer_only:
                pl.when(outer_piece(at))(message.start)
            else:
                message.start()
        return recv

    def send_block(k):
        last = k == W - 1
        send = last_send if last else bulk_send
        waves.append(over_plane(bulk_ref.at[k], rbulk_ref.at[k], send, last))

    maxima_send = stage(True)
    first_maxima = over_plane(m1_ref, r1_ref, maxima_send)
    sent.append((r1_ref, maxima_send))
    bulk_send, last_send = stage(True), stage(True)
    ahead = 3
    waves = []
    for k in range(ahead - 1):
        send_block(k)
    for k in range(W):
        rbulk_ref[k, here] = bulk_ref[k, y, x]

    diagonal = lax.broadcasted_iota(jnp.int32, (HAD, HAD), 0) == lax.broadcasted_iota(
        jnp.int32, (HAD, HAD), 1
    )
    for load in loads:
        load.wait()
    sign_row = signs_ref[...].astype(F32)
    signed_ref[...] = dot(
        jnp.where(diagonal, sign_row, 0.0).astype(BF16), table
    ).astype(BF16)
    for k in range(W):
        for i in range(3):
            adam_ref[i, k : k + 1, :] = state_ref[i, :, k * HAD : (k + 1) * HAD]

    landed(r1_ref, first_maxima)
    send_block(ahead - 1)
    peak = jnp.maximum(m1_ref[y, x], jnp.max(r1_ref[...], axis=0))
    m2_ref[...] = peak
    send, recv = stage(True), stage(False)
    copy(m2_ref, r2_ref, core_peer, send, recv).start()
    sent.append((r2_ref, send))
    landed(r2_ref, recv)
    peak = jnp.maximum(peak, r2_ref[...])
    m3_ref[...] = peak
    send, last_maxima = stage(True), stage(False)
    for j, o in enumerate(line):
        copy(m3_ref, r3_ref.at[j], line_peer[o], send, last_maxima).start()
    sent.append((r3_ref, send))

    signed = signed_ref[...]
    def rotate(k):
        value = rbulk_ref[k].reshape((here + 1) * pair, HAD)
        rot_ref[k] = dot(value, signed).reshape(here + 1, pair, HAD)

    for k in range(W - 1):
        landed(rbulk_ref.at[k, 0:here], waves[k])
        if k + ahead < W:
            send_block(k + ahead)
        rotate(k)

    outer = outer_piece(y)

    @pl.when(outer)
    def _():
        landed(rbulk_ref.at[W - 1, 0:here], waves[W - 1])
        rotate(W - 1)

    @pl.when(jnp.logical_not(outer))
    def _():
        rot_ref[W - 1] = jnp.zeros((here + 1, pair, HAD), F32)

    sent.append((rbulk_ref.at[0 : W - 1, 0:here], bulk_send))
    landed(r3_ref, last_maxima)
    peak = jnp.maximum(peak, jnp.max(r3_ref[...], axis=0))

    scales = jnp.sqrt(peak + 1e-06)
    inverse = 0.0625 / scales
    z_at = lax.broadcasted_iota(jnp.int32, (NZ, LANES), 0)
    l_at = lax.broadcasted_iota(jnp.int32, (NZ, LANES), 1)
    core_send = stage(True)
    core_recv = [stage(False) for _ in range(W)]
    for k in range(W):
        cols = slice(k * HAD, (k + 1) * HAD)
        pick = l_at == z_at * stride + k
        factor = jnp.concatenate(
            [
                jnp.sum(
                    jnp.where(pick, jnp.broadcast_to(inverse[g : g + 1], (NZ, LANES)), 0.0),
                    axis=1,
                    keepdims=True,
                )
                for g in range(CORES)
            ],
            axis=0,
        )
        factor = jnp.broadcast_to(factor, (pair, HAD))
        total = jnp.zeros((pair, HAD), F32)
        for j in range(here + 1):
            value = jnp.clip(rot_ref[k, j] * factor, -clip_level, clip_level)
            total = total + value.astype(BF16).astype(F32)
        acc_ref[0, :, cols] = total[0:NZ]
        acc_ref[1, :, cols] = total[NZ:pair]
        copy(
            acc_ref.at[1 - c, :, cols], racc_ref.at[:, cols], core_peer, core_send, core_recv[k]
        ).start()
    sent.append((racc_ref, core_send))

    w_at = lax.broadcasted_iota(jnp.int32, (W, LANES), 0)
    k_at = lax.broadcasted_iota(jnp.int32, (W, LANES), 1)
    own = jnp.broadcast_to(jnp.where(c == 0, scales[0:1], scales[1:2]), (W, LANES))
    own_scale = jnp.sum(
        jnp.where(k_at == z * stride + w_at, own, 0.0), axis=1, keepdims=True
    )

    for k in range(W):
        landed(racc_ref.at[:, k * HAD : (k + 1) * HAD], core_recv[k])
        for h in range(2):
            cols = slice(k * HAD + h * LANES, k * HAD + (h + 1) * LANES)
            zs_ref[:, h * W + k, :] = acc_ref[c, :, cols] + racc_ref[:, cols]

    send, recv = stage(True), stage(False)
    for j, o in enumerate(line):
        copy(zs_ref.at[lax.rem(z + o, NZ)], rz_ref.at[j], line_peer[o], send, recv).start()
    sent.append((rz_ref, send))
    own_part = zs_ref[z]
    landed(rz_ref, recv)
    total = own_part + jnp.sum(rz_ref[...], axis=0)

    wide = jnp.concatenate([total[0:W], total[W : 2 * W]], axis=1)
    parts = split_three(wide * own_scale)
    table = table_ref[...]
    gradient = (dot(parts[0], table) + dot(parts[1], table)) + dot(parts[2], table)
    gradient = gradient * 0.0625 * sign_row
    grad_ref[y] = gradient
    updated, _, _ = adam(gradient, adam_ref[0], adam_ref[1], adam_ref[2])
    updated = updated.astype(BF16).astype(F32)
    near_ref[len(near), 0:W] = updated[:, 0:LANES]
    near_ref[len(near), W : 2 * W] = updated[:, LANES:HAD]

    far_send, far_recv = stage(True), stage(False)
    near_send, near_recv = stage(True), stage(False)
    mine = near_ref.at[len(near)]
    slots = {o % NZ: (near_ref.at[i], near_send, near_recv) for i, o in enumerate(near)}
    slots.update({o % NZ: (far_ref.at[i], far_send, far_recv) for i, o in enumerate(far)})
    for o in line:
        slot, send, recv = slots[o]
        copy(mine, slot, line_peer[o], send, recv).start()
    sent.append((far_ref, far_send))
    if near:
        sent.append((near_ref.at[0 : len(near)], near_send))
    column_send, column_recv = stage(True), stage(False)
    for o in column:
        copy(
            grad_ref.at[y], grad_ref.at[y], device(0, o, 0, 0), column_send, column_recv
        ).start()
    sent.append((grad_ref.at[0 : NY - 1], column_send))

    WA = W // 2
    core_sends = (stage(True), stage(True))
    core_recvs = (stage(False), stage(False))
    step_sends = [[stage(True) for _ in range(2)] for _ in range(2)]
    sets = (ga_ref, gb_ref)
    extents = (NX, NY)

    def pack(wave, rows_ref):
        for k in range(W):
            both = jnp.concatenate([rows_ref[:, k, :], rows_ref[:, W + k, :]], axis=0)
            at = k if k < WA else k - WA
            sets[int(k >= WA)][c, wave, 0, :, at * LANES : (at + 1) * LANES] = both.astype(BF16)

    def along(wave, which, step):
        slots_ref = sets[which].at[c, wave]
        axis = which ^ step
        count = extents[which] if step else 1
        extent = extents[axis]
        send = step_sends[which][step]
        first = stage(False)
        recv = {}
        for o in sorted(range(1, extent), key=lambda o: -ring_distance(o, extent)):
            recv[o] = stage(False) if step and recv else first
            peer = device(o, 0, 0, 0) if axis == 0 else device(0, o, 0, 0)
            copy(
                slots_ref.at[0:count],
                slots_ref.at[count * o : count * (o + 1)],
                peer,
                send,
                recv[o],
            ).start()
        if wave and recv:
            sent.append((sets[which].at[c, :, count : count * extent], send))
        return recv

    def pass_on(which, piece):
        copy(piece, piece, core_peer, core_sends[which], core_recvs[which]).start()

    def arrive(wave, which, step, recv):
        slots_ref = sets[which].at[c, wave]
        if step == 0 and not recv:
            return
        if step == 0:
            landed(slots_ref.at[1 : len(recv) + 1], recv[1])
            return
        count = extents[which]
        for o in sorted(recv, key=lambda o: ring_distance(o, len(recv) + 1)):
            piece = slots_ref.at[count * o : count * (o + 1)]
            landed(piece, recv[o])
            pass_on(which, piece)

    if near:
        landed(near_ref.at[0 : len(near)], near_recv)
    pack(0, near_ref)
    near_one = [along(0, which, 0) for which in range(2)]
    landed(far_ref, far_recv)
    pack(1, far_ref)
    far_one = [along(1, which, 0) for which in range(2)]
    near_two = []
    far_two = []
    for which in range(2):
        arrive(0, which, 0, near_one[which])
        near_two.append(along(0, which, 1))
    for which in range(2):
        arrive(1, which, 0, far_one[which])
        far_two.append(along(1, which, 1))
    for wave in range(2):
        for which in range(2):
            pass_on(which, sets[which].at[c, wave, 0 : extents[which]])
    for which in range(2):
        arrive(0, which, 1, near_two[which])
    for which in range(2):
        arrive(1, which, 1, far_two[which])
    landed(grad_ref.at[0 : NY - 1], column_recv)
    for which in range(2):
        landed(sets[which].at[1 - c], core_recvs[which])
        sent.append((sets[which].at[c], core_sends[which]))

    for ref, index in sent:
        copy(ref, ref, core_peer, index, 0).wait_send()

    def last_sent(count):
        ref = rbulk_ref.at[W - 1, 0:count]
        copy(ref, ref, core_peer, last_send, 0).wait_send()

    pl.when(outer)(functools.partial(last_sent, 2 * NX - 1))
    pl.when(jnp.logical_not(outer))(functools.partial(last_sent, 2 * NX))


def write_kernel(
    sizes,
    ga_ref,
    gb_ref,
    grad_ref,
    master_ref,
    first_ref,
    second_ref,
    new_master_ref,
    new_first_ref,
    new_second_ref,
    out_hbm,
    adam_ref,
    out_ref,
    out_sems,
):
    NX, NY, NZ, NB, W = sizes
    rows = NX * NZ * CORES
    near, far = line_offsets(NZ)
    dp = lax.axis_index("dp")
    y = lax.axis_index("outer")
    z = lax.rem(dp // CORES, NZ)
    x = dp // (CORES * NZ)

    slots = rows
    deep = NZ // 2
    r_at = lax.broadcasted_iota(jnp.int32, (rows, slots), 0)
    g_at = lax.broadcasted_iota(jnp.int32, (1, slots), 1)
    low = lax.rem(g_at, deep)
    ox = lax.rem(g_at // deep, NX)
    part = lax.rem(g_at // (deep * NX), 2)
    core = g_at // (deep * NX * 2)
    back = max(NZ // 4 - 1, 0)
    near_o = jnp.where(low == len(near), 0, low - back + (low >= back).astype(jnp.int32))
    oz = jnp.where(part == 0, near_o, low + NZ // 2 - back)
    source = (lax.rem(x - ox + NX, NX) * NZ + lax.rem(z - oz + NZ, NZ)) * CORES + core
    pick = (r_at == source).astype(F32).astype(BF16)
    most = []
    lasts = []
    for oy in range(NY):
        at = lax.rem(y + NY - oy, NY)
        begin = piece_start(sizes, at) * HAD
        tiles = []
        for h in range(2):
            parts = []
            for which, ref in enumerate((ga_ref, gb_ref)):
                value = jnp.concatenate(
                    [
                        ref[
                            core,
                            wave,
                            ox * NY + oy if which else oy * NX + ox,
                            h * deep : (h + 1) * deep,
                        ]
                        for core in range(CORES)
                        for wave in range(2)
                        for ox in range(NX)
                    ],
                    axis=0,
                )
                parts.append(dot(pick, value).astype(BF16))
            tiles.append(jnp.concatenate(parts, axis=1))
        for k in range(W):
            both = jnp.concatenate(
                [tile[:, k * LANES : (k + 1) * LANES] for tile in tiles], axis=1
            )
            out_ref[oy, :, k * HAD : (k + 1) * HAD] = both
        kept = (W - 1) * HAD
        cols = pl.ds(pl.multiple_of(begin, HAD), kept)
        most.append(
            pltpu.make_async_copy(out_ref.at[oy, :, 0:kept], out_hbm.at[:, cols], out_sems.at[0, oy])
        )
        most[oy].start()
        cols = pl.ds(pl.multiple_of(begin + kept, HAD), HAD)
        last = pltpu.make_async_copy(
            out_ref.at[oy, :, kept : W * HAD], out_hbm.at[:, cols], out_sems.at[1, oy]
        )
        lasts.append(((at == 0) | (at == NY - 1), last))

        @pl.when(lasts[oy][0])
        def _():
            lasts[oy][1].start()

    for at in range(NY):
        begin = piece_start(sizes, at)
        for k in range(W):
            lo = (begin + k) * HAD
            adam_ref[0, k : k + 1, :] = master_ref[0:1, lo : lo + HAD]
            adam_ref[1, k : k + 1, :] = first_ref[0:1, lo : lo + HAD]
            adam_ref[2, k : k + 1, :] = second_ref[0:1, lo : lo + HAD]
        results = adam(grad_ref[at], adam_ref[0], adam_ref[1], adam_ref[2])
        end = piece_start(sizes, at + 1) if at < NY - 1 else NB
        for k in range(end - begin):
            lo = (begin + k) * HAD
            for ref, value in zip((new_master_ref, new_first_ref, new_second_ref), results):
                ref[0:1, lo : lo + HAD] = value[k : k + 1, :]

    for oy in range(NY):
        most[oy].wait()

        @pl.when(lasts[oy][0])
        def _():
            lasts[oy][1].wait()


def build(mesh, NX, NZ, NB):
    NY = mesh.shape["outer"]
    W = -(-NB // NY)
    sizes = (NX, NY, NZ, NB, W)
    rows = NX * NZ * CORES
    pair = CORES * NZ
    n_plane = NX * NY - 1
    n_line = NZ - 1
    sends = 16
    recvs = 10 + 2 * W + 4 + 2 * (NX + NY - 2)
    set_a = (W // 2) * LANES
    near, far = line_offsets(NZ)
    width = NB * HAD
    piece = W * HAD
    scratch = [
        pltpu.VMEM((rows, width), BF16),
        pltpu.VMEM((1, HAD), jnp.int32),
        pltpu.VMEM((3, 1, piece), F32),
        pltpu.VMEM((HAD, HAD), BF16),
        pltpu.VMEM((HAD, HAD), BF16),
        pltpu.VMEM((3, W, HAD), F32),
        pltpu.VMEM((W, NY, NX, pair, HAD), BF16),
        pltpu.VMEM((W, n_plane + 1, pair, HAD), BF16),
        pltpu.VMEM((W, n_plane + 1, pair, HAD), F32),
        pltpu.VMEM((NY, NX, CORES, LANES), F32),
        pltpu.VMEM((n_plane, CORES, LANES), F32),
        pltpu.VMEM((CORES, LANES), F32),
        pltpu.VMEM((CORES, LANES), F32),
        pltpu.VMEM((CORES, LANES), F32),
        pltpu.VMEM((n_line, CORES, LANES), F32),
        pltpu.VMEM((CORES, NZ, piece), F32),
        pltpu.VMEM((NZ, piece), F32),
        pltpu.VMEM((NZ, 2 * W, LANES), F32),
        pltpu.VMEM((n_line, 2 * W, LANES), F32),
        pltpu.VMEM((len(near) + 1, 2 * W, LANES), F32),
        pltpu.VMEM((len(far), 2 * W, LANES), F32),
        pltpu.SemaphoreType.DMA((5,)),
        pltpu.SemaphoreType.DMA((sends,)),
        pltpu.SemaphoreType.DMA((recvs,)),
    ]
    vmem = pl.BlockSpec(memory_space=pltpu.VMEM)
    row = jax.ShapeDtypeStruct((1, width), F32)

    def per_device(replica_grads, hadamard_signs, master_rows, first_moment, second_moment):
        first_set, second_set, gradients = pl.pallas_call(
            functools.partial(exchange_kernel, sizes),
            out_shape=(
                pltpu.VMEM((CORES, 2, n_plane + 1, NZ, set_a), BF16),
                pltpu.VMEM((CORES, 2, n_plane + 1, NZ, piece // 2 - set_a), BF16),
                pltpu.VMEM((NY, W, HAD), F32),
            ),
            in_specs=[pl.BlockSpec(memory_space=pltpu.HBM)] * 5,
            out_specs=(vmem, vmem, vmem),
            scratch_shapes=scratch,
            compiler_params=pltpu.CompilerParams(
                collective_id=0, has_side_effects=True, vmem_limit_bytes=40 * 2**20
            ),
        )(
            *[
                pltpu.with_memory_space_constraint(array, pltpu.HBM)
                for array in (
                    replica_grads,
                    hadamard_signs.reshape(1, HAD),
                    master_rows,
                    first_moment,
                    second_moment,
                )
            ]
        )
        return pl.pallas_call(
            functools.partial(write_kernel, sizes),
            out_shape=(row, row, row, jax.ShapeDtypeStruct((rows, width), BF16)),
            in_specs=[vmem] * 6,
            out_specs=(vmem,) * 3 + (pl.BlockSpec(memory_space=pl.ANY),),
            scratch_shapes=[
                pltpu.VMEM((3, W, HAD), F32),
                pltpu.VMEM((NY, rows, piece), BF16),
                pltpu.SemaphoreType.DMA((2, NY)),
            ],
            compiler_params=pltpu.CompilerParams(vmem_limit_bytes=20 * 2**20),
        )(first_set, second_set, gradients, master_rows, first_moment, second_moment)

    in_specs = (P("dp", "outer", None, None), P(), P("dp", None), P("dp", None), P("dp", None))
    out_specs = (P("dp", None), P("dp", None), P("dp", None), P())
    return jax.shard_map(
        per_device, mesh=mesh, in_specs=in_specs, out_specs=out_specs, check_vma=False
    )


def solution(mesh):
    return build(mesh, 4, 16, 18)
```
